256 devices in a mesh: gx: 4 (over y), gy: 8 (over z), gz: 8 (over x, core).
Axes of the slice: x: 4, y: 4, z: 8, core: 2. Of those that a mesh axis runs over, the one named last changes fastest.
Arguments:
- right_side: float32 [64, 256, 1024], P('gx', 'gy', 'gz'), may hold values from -6 to 6
- conductivity: float32 [64, 256, 1024], P('gx', 'gy', 'gz'), may hold values from 0.2 to 5
- screening: float32 [64, 256, 1024], P('gx', 'gy', 'gz'), may hold values from 0.01 to 0.2
Outputs:
- solution_field: float32 [64, 256, 1024], P('gx', 'gy', 'gz')
The draws below stay inside these ranges and needn't reach their ends.
All inputs are finite; a program needn't handle non-finite values.
Results may differ from the reference program's by a relative error of at most 0.0001.
Values sent between devices are 32-bit elements; how exact they have to be, the bound alone decides.
No kernel may reach another device: no remote copies, remote signals or barrier semaphores. Data moves between devices by JAX's collectives and lax.ppermute only.
A program may use at most 128 MiB of HBM per device.

```python
import math
import jax
import jax.numpy as jnp

SWEEPS = 2
COARSE_SWEEPS = 8
NX = 64
NY = 256
NZ = 1024


def draw_right_side(key, part):
    key = jax.random.fold_in(key, 11)
    values = jnp.clip(jax.random.normal(key, (NX, NY, NZ), jnp.float32), -6.0, 6.0)
    return values.astype(jnp.float32)


def shard_levels(rng, shape, pieces, smallest, largest):
    gain = 1.0
    for dim, shards_of in pieces:
        heights = jax.random.uniform(jax.random.fold_in(jax.random.fold_in(rng, 6), dim), (shards_of,), jnp.float32, smallest / len(pieces), largest / len(pieces))
        gain = gain * jnp.repeat(jnp.exp(heights), shape[dim] // shards_of).reshape((-1,) + (1,) * (len(shape) - 1 - dim))
    return gain


def setup_inputs(seed: int = 0) -> dict:
    seeds = jax.random.split(jax.random.key(seed), 4)
    return {
        "right_side": draw_right_side(jax.random.fold_in(seeds[3], 71), 0),
        "conductivity": jnp.clip(jnp.exp(math.log(5.0) - 3.218876 * jax.random.uniform(seeds[1], (NX, NY, NZ), jnp.float32) ** shard_levels(seeds[1], (NX, NY, NZ), ((0, 4), (1, 8), (2, 8)), -0.2, 0.2)), 0.2, 5.0),
        "screening": jnp.clip(jnp.exp(math.log(0.2) - 2.9957323 * jax.random.uniform(seeds[2], (NX, NY, NZ), jnp.float32) ** shard_levels(seeds[2], (NX, NY, NZ), ((0, 4), (1, 8), (2, 8)), -0.2, 0.2)), 0.01, 0.2),
    }


damping = 2.0 / 3.0


def neighbour_views():
    inner = slice(1, -1)
    return [(slice(2, None), inner, inner), (slice(0, -2), inner, inner),
            (inner, slice(2, None), inner), (inner, slice(0, -2), inner),
            (inner, inner, slice(2, None)), (inner, inner, slice(0, -2))]


def operate(field_pad, cond_pad, field, conduct, mass_term, spacing):
    result = mass_term * field
    diagonal = mass_term
    for window in neighbour_views():
        face_weight = spacing * 0.5 * (conduct + cond_pad[window])
        result = result + face_weight * (field - field_pad[window])
        diagonal = diagonal + face_weight
    return result, diagonal


def coarsen(field):
    return field.reshape(field.shape[0] // 2, 2, field.shape[1] // 2, 2, field.shape[2] // 2, 2).mean(axis=(1, 3, 5))


def refine(field):
    return jnp.repeat(jnp.repeat(jnp.repeat(field, 2, 0), 2, 1), 2, 2)


def smooth(field, source, cond_pad, conduct, mass_term, spacing):
    result, diagonal = operate(jnp.pad(field, 1), cond_pad, field, conduct, mass_term, spacing)
    return field + damping * (source - result) / diagonal


def reference(right_side, conductivity, screening):
    conducts = [conductivity]
    masses = [screening]
    for level_index in range(3):
        conducts.append(coarsen(conducts[level_index]))
        masses.append(coarsen(masses[level_index]))
    pads = [jnp.pad(item_cond, 1) for item_cond in conducts]
    sources = [right_side]
    fields = []
    for level_index in range(3):
        spacing = 0.25 ** level_index
        field = jnp.zeros_like(sources[level_index])
        for sweep_index in range(SWEEPS):
            field = smooth(field, sources[level_index], pads[level_index], conducts[level_index], masses[level_index], spacing)
        result, diagonal = operate(jnp.pad(field, 1), pads[level_index], field, conducts[level_index], masses[level_index], spacing)
        fields.append(field)
        sources.append(coarsen(sources[level_index] - result))
    field = jnp.zeros_like(sources[3])
    for sweep_index in range(COARSE_SWEEPS):
        field = smooth(field, sources[3], pads[3], conducts[3], masses[3], 0.25 ** 3)
    for level_index in (2, 1, 0):
        spacing = 0.25 ** level_index
        field = fields[level_index] + refine(field)
        for sweep_index in range(SWEEPS):
            field = smooth(field, sources[level_index], pads[level_index], conducts[level_index], masses[level_index], spacing)
    return field
```

```python
import functools

import jax
import jax.numpy as jnp
from jax import lax
from jax.experimental import pallas as pl
from jax.experimental.pallas import tpu as pltpu
from jax.sharding import PartitionSpec as P

SWEEPS = 2
COARSE_SWEEPS = 8
OMEGA = 2.0 / 3.0
KEEP = 1.0 - OMEGA
OUTSIDE = 1e30
LIMIT = 1e29
F32 = jnp.float32
HIGH = lax.Precision.HIGHEST


def dot(a, b):
    return jnp.dot(a, b, precision=HIGH, preferred_element_type=F32)


def iota(shape, dim):
    return lax.broadcasted_iota(jnp.int32, shape, dim)


def roll(x, shift, axis):
    size = x.shape[axis]
    shift = shift % size
    return x if shift == 0 else pltpu.roll(x, shift, axis)


def after(x, axis):
    return roll(x, -1, axis)


def before(x, axis):
    return roll(x, 1, axis)


def planes(low, high, body, unroll=2):
    def step(p, carry):
        body(p)
        return carry

    lax.fori_loop(low, high, step, 0, unroll=unroll)


def coefficients(low, high, spacing, k, f, m, d, w, g, cy, cz):
    half = 0.5 * spacing

    def body(p):
        here = k[p]
        y = half * (here + after(here, 0))
        z = half * (here + after(here, 1))
        diagonal = m[p] + half * (k[p - 1] + here) + half * (here + k[p + 1])
        diagonal = diagonal + y + before(y, 0) + z + before(z, 1)
        weight = jnp.where(m[p] < LIMIT, OMEGA / diagonal, 0.0)
        if d is not None:
            d[p] = diagonal
        w[p] = weight
        g[p] = weight * f[p]
        cy[p] = y
        cz[p] = z

    planes(low, high, body)


def neighbours(p, half, k, cy, cz, v):
    here, centre, y, z = k[p], v[p], cy[p], cz[p]
    total = half * (k[p - 1] + here) * v[p - 1] + half * (here + k[p + 1]) * v[p + 1]
    total = total + y * after(centre, 0) + before(y * centre, 0)
    total = total + z * after(centre, 1) + before(z * centre, 1)
    return total, centre


def sweep(low, high, spacing, k, w, g, cy, cz, v, out):
    half = 0.5 * spacing

    def body(p):
        total, centre = neighbours(p, half, k, cy, cz, v)
        out[p] = KEEP * centre + g[p] + w[p] * total

    planes(low, high, body)


def pack_y_kernel(f, k, m, xl, xr, up, down):
    for p in range(24):
        for out, lo3, lo4 in ((up, 29, 28), (down, 0, 0)):
            base = 10 * p
            if p < 4:
                kk = xl[6 + p, lo4 : lo4 + 4]
            elif p < 20:
                kk = k[p - 4, lo4 : lo4 + 4]
            else:
                kk = xr[6 + p - 20, lo4 : lo4 + 4]
            if 1 <= p < 4:
                ff, mm = xl[p - 1, lo3 : lo3 + 3], xl[2 + p, lo3 : lo3 + 3]
            elif 4 <= p < 20:
                ff, mm = f[p - 4, lo3 : lo3 + 3], m[p - 4, lo3 : lo3 + 3]
            elif 20 <= p < 23:
                ff, mm = xr[p - 20, lo3 : lo3 + 3], xr[p - 17, lo3 : lo3 + 3]
            else:
                ff = mm = jnp.zeros((3, 128), F32)
            out[base : base + 3] = ff
            out[base + 3 : base + 6] = mm
            out[base + 6 : base + 10] = kk


def pack_z_kernel(f, k, m, xl, xr, yl, yr, fa, ka, ma, up, down):
    lane = iota((40, 128), 1)
    zero = jnp.zeros((32, 128), F32)
    for g in range(2):
        acc_up = jnp.zeros((40, 128), F32)
        acc_down = jnp.zeros((40, 128), F32)
        for i in range(12):
            p = 12 * g + i
            base = 10 * p
            if p < 4:
                own = (xl[p - 1] if p else zero, xl[2 + p] if p else zero, xl[6 + p])
            elif p < 20:
                own = (f[p - 4], m[p - 4], k[p - 4])
            else:
                own = (xr[p - 20] if p < 23 else zero, xr[p - 17] if p < 23 else zero, xr[p - 14])
            for a, out in enumerate((fa, ma, ka)):
                width = 4 if a == 2 else 3
                out[p, 0:32] = own[a]
                out[p, 32:40] = jnp.zeros((8, 128), F32)
                out[p, 32 : 32 + width] = yr[base + 3 * a : base + 3 * a + width]
                out[p, 40 - width : 40] = yl[base + 3 * a : base + 3 * a + width]
                whole = out[p]
                first = 10 * i + 3 * a
                mask = (lane >= first) & (lane < first + width)
                acc_up = jnp.where(mask, roll(whole, first - (128 - width), 1), acc_up)
                acc_down = jnp.where(mask, roll(whole, first, 1), acc_down)
        up[g] = acc_up
        down[g] = acc_down


def pair_matrix(columns):
    return jnp.where(iota((128, columns), 0) // 2 == iota((128, columns), 1) % 64, 0.125, 0.0)


def fine_kernel(
    pos, fa, ka, ma, zl, zr, message, v_out, w, g, k, cy, cz, f, m, d, tall
):
    ix, iy, iz = pos[0], pos[1], pos[2]
    row = iota((40, 128), 0)
    lane = iota((40, 128), 1)
    far = ((row >= 32) & (row < 36) & (iy == 7)) | ((row >= 36) & (iy == 0))
    beside = ((lane < 4) & (iz < 7)) | ((lane >= 124) & (iz > 0))
    row_inner = (row < 35) | (row > 36)
    inner = (lane < 3) | (lane > 124)
    for p in range(24):
        group, i = p // 12, p % 12
        absent = False
        if p < 4:
            absent = ix == 0
        elif p >= 20:
            absent = ix == 3
        gone = far | absent
        for a, (src, out) in enumerate(((fa, f), (ma, m), (ka, k))):
            width = 4 if a == 2 else 3
            first = 10 * i + 3 * a
            right = roll(zr[group], -first, 1)
            left = roll(zl[group], 128 - width - first, 1)
            side = jnp.where(lane < 64, right, left)
            fill = OUTSIDE if a == 1 else 0.0
            if a == 1 and p in (0, 23):
                out[p] = jnp.full((40, 256), OUTSIDE, F32)
                continue
            if a == 2:
                here, there = gone, gone | ~beside
            else:
                here = gone | ~row_inner
                there = here | ~(beside & inner)
            out[p, :, 0:128] = jnp.where(here, fill, src[p])
            out[p, :, 128:256] = jnp.where(there, fill, side)
    coefficients(1, 23, 1.0, k, f, m, d, w, g, cy, cz)
    sweep(2, 22, 1.0, k, w, g, cy, cz, g, v_out)
    pairs = pair_matrix(128)
    lane16 = iota((16, 128), 1)

    def emit(slot, rows_of):
        for i in range(8):
            tall[32 * i : 32 * i + 32] = rows_of(2 * i + 4) + rows_of(2 * i + 5)
        halves = tall[pl.ds(0, 128, stride=2), :] + tall[pl.ds(1, 128, stride=2), :]
        coarse = dot(halves, pairs)
        for i in range(4):
            message[4 * slot + i] = jnp.where(
                lane16 < 64, coarse[16 * i : 16 * i + 16], coarse[16 * i + 64 : 16 * i + 80]
            )

    def residual(p):
        total, centre = neighbours(p, 0.5, k, cy, cz, v_out)
        return (f[p] + total - d[p] * centre)[0:32, 0:128]

    emit(0, residual)
    emit(1, lambda p: m[p, 0:32, 0:128])
    emit(2, lambda p: k[p, 0:32, 0:128])


def pack_z1_kernel(own, yl, yr, up, down):
    lane = iota((16, 128), 1) % 64
    for b in range(4):
        for a in range(3):
            for part, src in enumerate((own, yr, yl)):
                acc_up = jnp.zeros((16, 128), F32)
                acc_down = jnp.zeros((16, 128), F32)
                for q in range(4):
                    pair = src[12 * b + 4 * a + q]
                    mask = (lane >= 16 * q) & (lane < 16 * q + 16)
                    acc_up = jnp.where(mask, roll(pair, 16 * q - 48, 1), acc_up)
                    acc_down = jnp.where(mask, roll(pair, 16 * q, 1), acc_down)
                up[3 * b + a, 16 * part : 16 * part + 16] = acc_up
                down[3 * b + a, 16 * part : 16 * part + 16] = acc_down


def middle_kernel(
    pos, own, yl, yr, zl, zr,
    message, v1, w1, g1, k1, cy1, cz1, v2, w2, g2, k2, cy2, cz2,
    f1, m1, d1, f2, m2, d2, tall, small,
):
    ix, iy, iz = pos[0], pos[1], pos[2]
    row = iota((48, 128), 0)
    lane = iota((48, 128), 1)
    gone = ((row >= 16) & (row < 32) & (iy == 7)) | ((row >= 32) & (iy == 0))
    gone = gone | ((lane >= 64) & (lane < 80) & (iz == 7)) | ((lane >= 112) & (iz == 0))
    gone = gone | ((lane >= 80) & (lane < 112))
    for ref in (k1, g1, v1, k2, g2, v2):
        ref[0] = jnp.zeros(ref.shape[1:], F32)
        ref[ref.shape[0] - 1] = jnp.zeros(ref.shape[1:], F32)
    for b in range(4):
        block = 8 * jnp.bitwise_xor(ix, b) + 1
        for a, (out, fill) in enumerate(((f1, 0.0), (m1, OUTSIDE), (k1, 0.0))):
            left, right = zl[3 * b + a], zr[3 * b + a]
            for q in range(4):
                s = 12 * b + 4 * a + q
                pair = jnp.concatenate([own[s], yr[s], yl[s]], axis=0)
                for h in range(2):
                    at = 16 * (q + 4 * h)
                    side = jnp.where(lane < 96, roll(right, 64 - at, 1), roll(left, 112 - at, 1))
                    value = jnp.where(lane < 64, roll(pair, 64 * h, 1), side)
                    out[block + q + 4 * h] = jnp.where(gone, fill, value)
    coefficients(1, 33, 0.25, k1, f1, m1, d1, w1, g1, cy1, cz1)
    sweep(1, 33, 0.25, k1, w1, g1, cy1, cz1, g1, v1)

    column = iota((128, 128), 1)
    known = (column < 40) | (column >= 120)
    pairs = jnp.where(known, pair_matrix(128), 0.0)
    lane24 = iota((24, 128), 1)
    unknown = (lane24 >= 40) & (lane24 < 120)

    def to_second(out, value_of, fill):
        for i in range(16):
            tall[48 * i : 48 * i + 48] = value_of(2 * i + 1) + value_of(2 * i + 2)
        halves = tall[pl.ds(0, 384, stride=2), :] + tall[pl.ds(1, 384, stride=2), :]
        coarse = dot(halves, pairs)
        for i in range(16):
            out[i + 1] = jnp.where(unknown, fill, coarse[24 * i : 24 * i + 24])

    def residual1(p):
        total, centre = neighbours(p, 0.125, k1, cy1, cz1, v1)
        return jnp.where(gone, 0.0, f1[p] + total - d1[p] * centre)

    to_second(f2, residual1, 0.0)
    to_second(m2, lambda p: m1[p], OUTSIDE)
    to_second(k2, lambda p: k1[p], 0.0)
    coefficients(1, 17, 0.0625, k2, f2, m2, d2, w2, g2, cy2, cz2)
    sweep(1, 17, 0.0625, k2, w2, g2, cy2, cz2, g2, v2)

    spread = jnp.where(iota((128, 128), 0) // 2 == column % 16, 0.125, 0.0)
    group = iota((12, 128), 1) // 16

    def to_third(slot, value_of):
        for i in range(8):
            tall[24 * i : 24 * i + 24] = value_of(2 * i + 1) + value_of(2 * i + 2)
        halves = tall[pl.ds(0, 96, stride=2), :] + tall[pl.ds(1, 96, stride=2), :]
        small[0:96] = dot(halves, spread)
        packed = jnp.zeros((12, 128), F32)
        for i in range(8):
            packed = jnp.where(group == i, small[12 * i : 12 * i + 12], packed)
        small[0:12] = packed
        message[slot, 0:2] = small[10:12]
        message[slot, 2:8] = small[0:6]

    row24 = iota((24, 128), 0)
    gone2 = ((row24 >= 8) & (row24 < 16) & (iy == 7)) | ((row24 >= 16) & (iy == 0))

    def residual2(p):
        total, centre = neighbours(p, 0.03125, k2, cy2, cz2, v2)
        return jnp.where(gone2, 0.0, f2[p] + total - d2[p] * centre)

    to_third(0, residual2)
    to_third(1, lambda p: m2[p])
    to_third(2, lambda p: k2[p])


def last_kernel(
    pos, own, first, second, v0, w0, g0, k0, cy0, cz0, v1, w1, g1, k1, cy1, cz1, v2, w2, g2, k2, cy2, cz2,
    out,
    k3, f3, m3, w3, g3, cy3, cz3, a3, b3, rows, dup, a2, b2, a1, b1, wide, low, high, a0, b0,
):
    ix, iy, iz = pos[0], pos[1], pos[2]
    row = iota((24, 128), 0) + 4 * iy - 10
    lane = iota((24, 128), 1)
    gone = (row < 0) | (row >= 32) | ((lane >= 32) & (lane < 112))
    gone = gone | ((lane >= 16) & (lane < 32) & (iz == 7)) | ((lane >= 112) & (iz == 0))
    for ref in (k3, g3, a3, b3, a2, b2, a1, b1):
        ref[0] = jnp.zeros(ref.shape[1:], F32)
        ref[ref.shape[0] - 1] = jnp.zeros(ref.shape[1:], F32)
    crossed = (iy == 2) | (iy == 6)

    def stack(index):
        one, two = first[index], second[index]
        ahead, behind = jnp.where(crossed, two, one), jnp.where(crossed, one, two)
        ahead = jnp.where(iy == 1, roll(ahead, 4, 0), ahead)
        behind = jnp.where(iy == 6, roll(behind, 4, 0), behind)
        return jnp.concatenate([ahead, own[index], behind], axis=0)

    for a, (ref, fill) in enumerate(((f3, 0.0), (m3, OUTSIDE), (k3, 0.0))):
        here, left, right = (stack(3 * z + a) for z in range(3))
        for x in range(8):
            value = jnp.where(
                lane < 16,
                roll(here, -16 * x, 1),
                jnp.where(lane < 64, roll(right, 16 - 16 * x, 1), roll(left, 112 - 16 * x, 1)),
            )
            ref[x + 1] = jnp.where(gone, fill, value)
    spacing = 0.25**3
    coefficients(1, 9, spacing, k3, f3, m3, None, w3, g3, cy3, cz3)
    source = g3
    for index in range(COARSE_SWEEPS - 1):
        target = (a3, b3)[index % 2]
        sweep(1, 9, spacing, k3, w3, g3, cy3, cz3, source, target)
        source = target

    src, column = iota((128, 128), 0), iota((128, 128), 1)
    to2 = jnp.where(
        ((column < 40) & (src == column // 2)) | ((column >= 120) & (src == 64 + column // 2)), 1.0, 0.0
    )
    for x in range(8):
        rows[24 * x : 24 * x + 24] = source[x + 1]
    rows[0:192] = dot(rows[0:192], to2)
    for x in range(8):
        dup[0:24] = jnp.zeros((24, 128), F32)
        mid = rows[24 * x + 10 : 24 * x + 16]
        dup[pl.ds(0, 6, stride=2), :] = mid
        dup[pl.ds(1, 6, stride=2), :] = mid
        ahead = rows[24 * x + 8 : 24 * x + 10]
        dup[pl.ds(20, 2, stride=2), :] = ahead
        dup[pl.ds(21, 2, stride=2), :] = ahead
        both = dup[0:24]
        a2[2 * x + 1] = v2[2 * x + 1] + both
        a2[2 * x + 2] = v2[2 * x + 2] + both
    sweep(1, 17, 0.0625, k2, w2, g2, cy2, cz2, a2, b2)
    sweep(1, 17, 0.0625, k2, w2, g2, cy2, cz2, b2, a2)

    to1 = jnp.where(
        ((column < 80) & (src == column // 2)) | ((column >= 112) & (src == 64 + column // 2)), 1.0, 0.0
    )
    for x in range(16):
        rows[24 * x : 24 * x + 24] = a2[x + 1]
    fine = dot(rows[0:384], to1)
    dup[pl.ds(0, 384, stride=2), :] = fine
    dup[pl.ds(1, 384, stride=2), :] = fine
    for x in range(16):
        both = dup[48 * x : 48 * x + 48]
        a1[2 * x + 1] = v1[2 * x + 1] + both
        a1[2 * x + 2] = v1[2 * x + 2] + both
    sweep(1, 33, 0.25, k1, w1, g1, cy1, cz1, a1, b1)
    sweep(1, 33, 0.25, k1, w1, g1, cy1, cz1, b1, a1)

    to0 = jnp.where(iota((128, 256), 0) == iota((128, 256), 1) // 2, 1.0, 0.0)
    for x in range(10):
        rows[48 * x : 48 * x + 48] = a1[8 * ix + x]
    wide[...] = dot(rows[0:480], to0)
    for x in range(10):
        for half, lanes in ((low, slice(0, 128)), (high, slice(128, 256))):
            mid = wide[48 * x : 48 * x + 18, lanes]
            half[pl.ds(0, 18, stride=2), :] = mid
            half[pl.ds(1, 18, stride=2), :] = mid
            ahead = wide[48 * x + 46 : 48 * x + 48, lanes]
            half[pl.ds(36, 2, stride=2), :] = ahead
            half[pl.ds(37, 2, stride=2), :] = ahead
            for p in (2 * x + 2, 2 * x + 3):
                a0[p, :, lanes] = v0[p, :, lanes] + half[...]
    sweep(3, 21, 1.0, k0, w0, g0, cy0, cz0, a0, b0)

    def body(p):
        total, centre = neighbours(p, 0.5, k0, cy0, cz0, b0)
        value = KEEP * centre + g0[p] + w0[p] * total
        out[p - 4] = value[0:32, 0:128]

    planes(4, 20, body)


VMEM = pl.BlockSpec(memory_space=pltpu.VMEM)
SMEM = pl.BlockSpec(memory_space=pltpu.SMEM)


COARSE_TARGETS = ((1, 3, 4, 5, 2, 7, 0, 6), (2, 7, 0, 1, 6, 3, 4, 5))


def call(kernel, outs, scratch, *args, pos=None):
    specs = [VMEM] * len(args)
    if pos is not None:
        args = (pos,) + args
        specs = [SMEM] + specs
    return pl.pallas_call(
        kernel,
        out_shape=[jax.ShapeDtypeStruct(s, F32) for s in outs],
        in_specs=specs,
        out_specs=[VMEM] * len(outs),
        scratch_shapes=[pltpu.VMEM(s, F32) for s in scratch],
        compiler_params=pltpu.CompilerParams(vmem_limit_bytes=48 * 1024 * 1024),
        name=kernel.__name__,
    )(*args)


def shift(x, axis, step):
    size = lax.axis_size(axis)
    return lax.ppermute(x, axis, [(i, (i + step) % size) for i in range(size)])


def swap(x, axis, bits):
    size = lax.axis_size(axis)
    return lax.ppermute(x, axis, [(i, i ^ bits) for i in range(size)])


def per_device(f, k, m):
    pos = jnp.stack([lax.axis_index("gx"), lax.axis_index("gy"), lax.axis_index("gz")])
    pos = pos.astype(jnp.int32)
    xl = shift(jnp.concatenate([f[13:], m[13:], k[12:]]), "gx", 1)
    xr = shift(jnp.concatenate([f[:3], m[:3], k[:4]]), "gx", -1)
    up, down = call(pack_y_kernel, [(240, 128)] * 2, [], f, k, m, xl, xr)
    yl, yr = shift(up, "gy", 1), shift(down, "gy", -1)
    fa, ka, ma, up, down = call(
        pack_z_kernel, [(24, 40, 128)] * 3 + [(2, 40, 128)] * 2, [], f, k, m, xl, xr, yl, yr
    )
    zl, zr = shift(up, "gz", 1), shift(down, "gz", -1)
    full = (24, 40, 256)
    message, *level0 = call(
        fine_kernel,
        [(12, 16, 128)] + [full] * 6,
        [full] * 3 + [(256, 128)],
        fa, ka, ma, zl, zr,
        pos=pos,
    )
    own = jnp.concatenate([message] + [swap(message, "gx", bits) for bits in (1, 2, 3)])
    yl, yr = shift(own, "gy", 1), shift(own, "gy", -1)
    up, down = call(pack_z1_kernel, [(12, 48, 128)] * 2, [], own, yl, yr)
    zl, zr = shift(up, "gz", 1), shift(down, "gz", -1)
    one, two = (34, 48, 128), (18, 24, 128)
    message, *rest = call(
        middle_kernel,
        [(3, 8, 128)] + [one] * 6 + [two] * 6,
        [one] * 3 + [two] * 3 + [(768, 128), (96, 128)],
        own, yl, yr, zl, zr,
        pos=pos,
    )
    level1, level2 = rest[:6], rest[6:]
    own = jnp.concatenate([message, shift(message, "gz", 1), shift(message, "gz", -1)])
    first, second = (lax.ppermute(own, "gy", list(enumerate(t))) for t in COARSE_TARGETS)
    three = (10, 24, 128)
    return call(
        last_kernel,
        [(16, 32, 128)],
        [three] * 9 + [(480, 128), (768, 128)] + [two] * 2 + [one] * 2
        + [(480, 256), (40, 128), (40, 128)] + [full] * 2,
        own, first, second, *level0, *level1, *level2,
        pos=pos,
    )[0]


def solution(mesh):
    placed = (P("gx", "gy", "gz"), P("gx", "gy", "gz"), P("gx", "gy", "gz"))
    return jax.shard_map(
        per_device, mesh=mesh, in_specs=placed, out_specs=P("gx", "gy", "gz"), check_vma=False
    )
```

```python
import functools

import jax
import jax.numpy as jnp
from jax import lax
from jax.experimental import pallas as pl
from jax.experimental.pallas import tpu as pltpu
from jax.sharding import PartitionSpec as P

SWEEPS = 2
COARSE_SWEEPS = 8
OMEGA = 2.0 / 3.0
KEEP = 1.0 - OMEGA
OUTSIDE = 1e30
LIMIT = 1e29
F32 = jnp.float32
BF16 = jnp.bfloat16


def dot(a, b):
    high = a.astype(BF16)
    rest = a - high.astype(F32)
    middle = rest.astype(BF16)
    low = (rest - middle.astype(F32)).astype(BF16)
    terms = jnp.concatenate([high, middle, low], axis=1)
    matrix = b.astype(BF16)
    return jnp.dot(terms, jnp.concatenate([matrix] * 3, axis=0), preferred_element_type=F32)


def iota(shape, dim):
    return lax.broadcasted_iota(jnp.int32, shape, dim)


def roll(x, shift, axis):
    size = x.shape[axis]
    shift = shift % size
    return x if shift == 0 else pltpu.roll(x, shift, axis)


def after(x, axis):
    return roll(x, -1, axis)


def before(x, axis):
    return roll(x, 1, axis)


def planes(low, high, values, store, group):
    def run(first, count):
        found = [values(first + i) for i in range(count)]
        for i, value in enumerate(found):
            store(first + i, value)

    whole = (high - low) // group
    if whole == 1:
        run(low, group)
    elif whole:

        def step(index, carry):
            run(low + index * group, group)
            return carry

        lax.fori_loop(0, whole, step, 0)
    if (high - low) % group:
        run(low + whole * group, (high - low) % group)


def coefficients(low, high, group, k, f, m, d, w, g, cy, cz):
    def values(p):
        here = k[p]
        y = here + after(here, 0)
        z = here + after(here, 1)
        diagonal = m[p] + (k[p - 1] + here) + (here + k[p + 1])
        diagonal = diagonal + y + before(y, 0) + z + before(z, 1)
        weight = jnp.where(m[p] < LIMIT, OMEGA / diagonal, 0.0)
        return y, z, weight, diagonal, None if f is None else weight * f[p]

    def store(p, found):
        cy[p], cz[p], w[p] = found[:3]
        if d is not None:
            d[p] = found[3]
        if f is not None:
            g[p] = found[4]

    planes(low, high, values, store, group)


def neighbours(p, k, cy, cz, v):
    here, centre, y, z = k[p], v[p], cy[p], cz[p]
    total = (k[p - 1] + here) * v[p - 1] + (here + k[p + 1]) * v[p + 1]
    total = total + y * after(centre, 0) + before(y * centre, 0)
    total = total + z * after(centre, 1) + before(z * centre, 1)
    return total, centre


def sweep(low, high, group, k, w, g, cy, cz, v, out):
    def values(p):
        total, centre = neighbours(p, k, cy, cz, v)
        return KEEP * centre + g[p] + w[p] * total

    def store(p, value):
        out[p] = value

    planes(low, high, values, store, group)


def pack_y_kernel(f, k, m, xl, xr, up, down):
    for p in range(24):
        for out, lo3, lo4 in ((up, 29, 28), (down, 0, 0)):
            base = 10 * p
            if p < 4:
                kk = xl[6 + p, lo4 : lo4 + 4]
            elif p < 20:
                kk = k[p - 4, lo4 : lo4 + 4]
            else:
                kk = xr[6 + p - 20, lo4 : lo4 + 4]
            if 1 <= p < 4:
                ff, mm = xl[p - 1, lo3 : lo3 + 3], xl[2 + p, lo3 : lo3 + 3]
            elif 4 <= p < 20:
                ff, mm = f[p - 4, lo3 : lo3 + 3], m[p - 4, lo3 : lo3 + 3]
            elif 20 <= p < 23:
                ff, mm = xr[p - 20, lo3 : lo3 + 3], xr[p - 17, lo3 : lo3 + 3]
            else:
                ff = mm = jnp.zeros((3, 128), F32)
            out[base : base + 3] = ff
            out[base + 3 : base + 6] = mm
            out[base + 6 : base + 10] = kk


def pack_z_kernel(f, k, m, xl, xr, yl, yr, fa, ka, ma, up, down):
    lane = iota((40, 128), 1)
    zero = jnp.zeros((32, 128), F32)
    for g in range(2):
        acc_up = jnp.zeros((40, 128), F32)
        acc_down = jnp.zeros((40, 128), F32)
        for i in range(12):
            p = 12 * g + i
            base = 10 * p
            if p < 4:
                own = (xl[p - 1] if p else zero, xl[2 + p] if p else zero, xl[6 + p])
            elif p < 20:
                own = (f[p - 4], m[p - 4], k[p - 4])
            else:
                own = (xr[p - 20] if p < 23 else zero, xr[p - 17] if p < 23 else zero, xr[p - 14])
            for a, out in enumerate((fa, ma, ka)):
                width = 4 if a == 2 else 3
                out[p, 0:32] = own[a]
                out[p, 32:40] = jnp.zeros((8, 128), F32)
                out[p, 32 : 32 + width] = yr[base + 3 * a : base + 3 * a + width]
                out[p, 40 - width : 40] = yl[base + 3 * a : base + 3 * a + width]
                whole = out[p]
                first = 10 * i + 3 * a
                mask = (lane >= first) & (lane < first + width)
                acc_up = jnp.where(mask, roll(whole, first - (128 - width), 1), acc_up)
                acc_down = jnp.where(mask, roll(whole, first, 1), acc_down)
        up[g] = acc_up
        down[g] = acc_down


def pair_matrix(columns):
    return jnp.where(iota((128, columns), 0) // 2 == iota((128, columns), 1) % 64, 0.125, 0.0)


def coarse_kernel(k, m, message, tall):
    pairs = pair_matrix(128)
    for slot, ref in enumerate((m, k)):
        for i in range(8):
            tall[32 * i : 32 * i + 32] = ref[2 * i] + ref[2 * i + 1]
        halve_and_pack(tall, pairs, message, 4 * slot)


def halve_and_pack(tall, pairs, message, first):
    lane16 = iota((16, 128), 1)
    halves = tall[pl.ds(0, 128, stride=2), :] + tall[pl.ds(1, 128, stride=2), :]
    coarse = dot(halves, pairs)
    for i in range(4):
        message[first + i] = jnp.where(
            lane16 < 64, coarse[16 * i : 16 * i + 16], coarse[16 * i + 64 : 16 * i + 80]
        )


def fine_kernel(pos, fa, ka, ma, zl, zr, message, v_out, w, g, k, cy, cz, f, m, d, tall):
    ix, iy, iz = pos[0], pos[1], pos[2]
    row = iota((40, 128), 0)
    lane = iota((40, 128), 1)
    far = ((row >= 32) & (row < 36) & (iy == 7)) | ((row >= 36) & (iy == 0))
    beside = ((lane < 4) & (iz < 7)) | ((lane >= 124) & (iz > 0))
    row_inner = (row < 35) | (row > 36)
    inner = (lane < 3) | (lane > 124)
    for p in range(24):
        group, i = p // 12, p % 12
        absent = False
        if p < 4:
            absent = ix == 0
        elif p >= 20:
            absent = ix == 3
        gone = far | absent
        for a, (src, out) in enumerate(((fa, f), (ma, m), (ka, k))):
            width = 4 if a == 2 else 3
            first = 10 * i + 3 * a
            if a == 1 and p in (0, 23):
                out[p] = jnp.full((40, 256), OUTSIDE, F32)
                continue
            right = roll(zr[group], -first, 1)
            left = roll(zl[group], 128 - width - first, 1)
            side = jnp.where(lane < 64, right, left)
            own = src[p]
            fill = OUTSIDE if a == 1 else 0.0
            if a == 2:
                here, there = gone, gone | ~beside
                own, side = 0.5 * own, 0.5 * side
            else:
                here = gone | ~row_inner
                there = here | ~(beside & inner)
            out[p, :, 0:128] = jnp.where(here, fill, own)
            out[p, :, 128:256] = jnp.where(there, fill, side)
    coefficients(1, 23, 4, k, f, m, d, w, g, cy, cz)
    sweep(2, 22, 4, k, w, g, cy, cz, g, v_out)

    def residual(p):
        total, centre = neighbours(p, k, cy, cz, v_out)
        return (f[p] + total - d[p] * centre)[0:32, 0:128]

    def values(i):
        return residual(2 * i + 4) + residual(2 * i + 5)

    def store(i, value):
        tall[pl.ds(pl.multiple_of(32 * i, 32), 32), :] = value

    planes(0, 8, values, store, 2)
    halve_and_pack(tall, pair_matrix(128), message, 0)


def pack_z1_kernel(count, own, yl, yr, up, down):
    lane = iota((16, 128), 1) % 64
    for b in range(4 * count):
        for part, src in enumerate((own, yr, yl)):
            acc_up = jnp.zeros((16, 128), F32)
            acc_down = jnp.zeros((16, 128), F32)
            for q in range(4):
                pair = src[4 * b + q]
                mask = (lane >= 16 * q) & (lane < 16 * q + 16)
                acc_up = jnp.where(mask, roll(pair, 16 * q - 48, 1), acc_up)
                acc_down = jnp.where(mask, roll(pair, 16 * q, 1), acc_down)
            up[b, 16 * part : 16 * part + 16] = acc_up
            down[b, 16 * part : 16 * part + 16] = acc_down


def clear(refs, low, high):
    for ref in refs:
        for p in (*range(low), *range(high, ref.shape[0])):
            ref[p] = jnp.zeros(ref.shape[1:], F32)


def outside1(iy, iz):
    row, lane = iota((48, 128), 0), iota((48, 128), 1)
    gone = ((row >= 16) & (row < 32) & (iy == 7)) | ((row >= 32) & (iy == 0))
    gone = gone | ((lane >= 64) & (lane < 80) & (iz == 7)) | ((lane >= 112) & (iz == 0))
    return gone | ((lane >= 80) & (lane < 112))


def spread1(ix, gone, own, yl, yr, zl, zr, count, a, out, fill, scale):
    lane = iota((48, 128), 1)
    for b in range(4):
        block = 8 * jnp.bitwise_xor(ix, b) + 4
        left, right = zl[count * b + a], zr[count * b + a]
        for q in range(4):
            s = 4 * (count * b + a) + q
            pair = jnp.concatenate([own[s], yr[s], yl[s]], axis=0)
            for h in range(2):
                at = 16 * (q + 4 * h)
                side = jnp.where(lane < 96, roll(right, 64 - at, 1), roll(left, 112 - at, 1))
                value = jnp.where(lane < 64, roll(pair, 64 * h, 1), side)
                value = value if scale == 1.0 else scale * value
                out[block + q + 4 * h] = jnp.where(gone, fill, value)


def known2(shape):
    lane = iota(shape, 1)
    return (lane < 40) | (lane >= 120)


def to_second(tall, out, values, fill):
    def store(i, value):
        tall[pl.ds(pl.multiple_of(48 * i, 48), 48), :] = value

    planes(0, 16, lambda i: values(2 * i + 4) + values(2 * i + 5), store, 4)
    halves = tall[pl.ds(0, 384, stride=2), :] + tall[pl.ds(1, 384, stride=2), :]
    coarse = dot(halves, jnp.where(known2((128, 128)), pair_matrix(128), 0.0))
    for i in range(16):
        out[i + 4] = jnp.where(known2((24, 128)), coarse[24 * i : 24 * i + 24], fill)


def to_third(tall, small, write, values):
    for i in range(8):
        tall[24 * i : 24 * i + 24] = values(2 * i + 4) + values(2 * i + 5)
    halves = tall[pl.ds(0, 96, stride=2), :] + tall[pl.ds(1, 96, stride=2), :]
    spread = jnp.where(iota((128, 128), 0) // 2 == iota((128, 128), 1) % 16, 0.125, 0.0)
    small[0:96] = dot(halves, spread)
    group = iota((12, 128), 1) // 16
    packed = jnp.zeros((12, 128), F32)
    for i in range(8):
        packed = jnp.where(group == i, small[12 * i : 12 * i + 12], packed)
    small[0:12] = packed
    write(slice(0, 2), small[10:12])
    write(slice(2, 8), small[0:6])


def cut1(ix, src, out):
    for p in range(16):
        out[p, 0:20] = src[8 * ix + p, 0:20]
        out[p, 20:24] = src[8 * ix + p, 44:48]


def cut2(ix, src, out):
    for p in range(12):
        out[p, 0:12] = src[4 * ix + p, 0:12]
        out[p, 12:16] = src[4 * ix + p, 20:24]


def static_kernel(
    pos, own, yl, yr, zl, zr,
    coarsest, k1, w1, cy1, cz1, d1, k2, w2, cy2, cz2, d2,
    k1n, w1n, cy1n, cz1n, k2n, w2n, cy2n, cz2n,
    m1, m2, tall, small,
):
    ix, iy, iz = pos[0], pos[1], pos[2]
    gone = outside1(iy, iz)
    clear((k1, w1, cy1, cz1), 4, 36)
    clear((k2, w2, cy2, cz2), 4, 20)
    spread1(ix, gone, own, yl, yr, zl, zr, 2, 0, m1, OUTSIDE, 1.0)
    spread1(ix, gone, own, yl, yr, zl, zr, 2, 1, k1, 0.0, 0.125)
    coefficients(4, 36, 8, k1, None, m1, d1, w1, None, cy1, cz1)
    to_second(tall, m2, lambda p: m1[p], OUTSIDE)
    to_second(tall, k2, lambda p: 0.25 * k1[p], 0.0)
    coefficients(4, 20, 8, k2, None, m2, d2, w2, None, cy2, cz2)

    def write(slot):
        def put(where, value):
            coarsest[slot, where] = value

        return put

    to_third(tall, small, write(0), lambda p: m2[p])
    to_third(tall, small, write(1), lambda p: 0.25 * k2[p])
    for src, out in ((k1, k1n), (w1, w1n), (cy1, cy1n), (cz1, cz1n)):
        cut1(ix, src, out)
    for src, out in ((k2, k2n), (w2, w2n), (cy2, cy2n), (cz2, cz2n)):
        cut2(ix, src, out)


def middle_kernel(
    pos, own, yl, yr, zl, zr, coarsest, k1, w1, cy1, cz1, d1, k2, w2, cy2, cz2, d2,
    message, v1n, g1n, v2n, g2n,
    f1, g1, v1, f2, g2, v2, tall, small,
):
    ix, iy, iz = pos[0], pos[1], pos[2]
    gone = outside1(iy, iz)
    clear((g1, v1), 4, 36)
    clear((g2, v2), 4, 20)
    spread1(ix, gone, own, yl, yr, zl, zr, 1, 0, f1, 0.0, 1.0)

    def weigh(low, high, w, f, g):
        def store(p, value):
            g[p] = value

        planes(low, high, lambda p: w[p] * f[p], store, 8)

    weigh(4, 36, w1, f1, g1)
    sweep(4, 36, 8, k1, w1, g1, cy1, cz1, g1, v1)

    def residual1(p):
        total, centre = neighbours(p, k1, cy1, cz1, v1)
        return jnp.where(gone, 0.0, f1[p] + total - d1[p] * centre)

    to_second(tall, f2, residual1, 0.0)
    weigh(4, 20, w2, f2, g2)
    sweep(4, 20, 8, k2, w2, g2, cy2, cz2, g2, v2)
    row24 = iota((24, 128), 0)
    gone2 = ((row24 >= 8) & (row24 < 16) & (iy == 7)) | ((row24 >= 16) & (iy == 0))

    def residual2(p):
        total, centre = neighbours(p, k2, cy2, cz2, v2)
        return jnp.where(gone2, 0.0, f2[p] + total - d2[p] * centre)

    def put(where, value):
        message[0, where] = value

    to_third(tall, small, put, residual2)
    message[1] = coarsest[0]
    message[2] = coarsest[1]
    cut1(ix, v1, v1n)
    cut1(ix, g1, g1n)
    cut2(ix, v2, v2n)
    cut2(ix, g2, g2n)


def duplicate(out, base, rows, first, count):
    value = rows[first : first + count]
    out[pl.ds(base, count, stride=2), :] = value
    out[pl.ds(base + 1, count, stride=2), :] = value


def last_kernel(
    pos, own, first, second, v0, w0, g0, k0, cy0, cz0, v1, g1, v2, g2, k1, w1, cy1, cz1, k2, w2, cy2, cz2,
    out,
    k3, f3, m3, w3, g3, cy3, cz3, a3, b3, rows, dup, a2, b2, a1, b1, wide, low, high, a0, b0,
):
    ix, iy, iz = pos[0], pos[1], pos[2]
    row = iota((24, 128), 0) + 4 * iy - 10
    lane = iota((24, 128), 1)
    gone = (row < 0) | (row >= 32) | ((lane >= 32) & (lane < 112))
    gone = gone | ((lane >= 16) & (lane < 32) & (iz == 7)) | ((lane >= 112) & (iz == 0))
    clear((k3, g3, a3, b3), 2, 10)
    crossed = (iy == 2) | (iy == 6)

    def stack(index):
        one, two = first[index], second[index]
        ahead, behind = jnp.where(crossed, two, one), jnp.where(crossed, one, two)
        ahead = jnp.where(iy == 1, roll(ahead, 4, 0), ahead)
        behind = jnp.where(iy == 6, roll(behind, 4, 0), behind)
        return jnp.concatenate([ahead, own[index], behind], axis=0)

    for a, (ref, fill) in enumerate(((f3, 0.0), (m3, OUTSIDE), (k3, 0.0))):
        here, left, right = (stack(3 * z + a) for z in range(3))
        for x in range(8):
            value = jnp.where(
                lane < 16,
                roll(here, -16 * x, 1),
                jnp.where(lane < 64, roll(right, 16 - 16 * x, 1), roll(left, 112 - 16 * x, 1)),
            )
            ref[x + 2] = jnp.where(gone, fill, value)
    coefficients(2, 10, 8, k3, f3, m3, None, w3, g3, cy3, cz3)
    source = g3
    for index in range(COARSE_SWEEPS - 1):
        target = (a3, b3)[index % 2]
        sweep(2, 10, 8, k3, w3, g3, cy3, cz3, source, target)
        source = target

    src, column = iota((128, 128), 0), iota((128, 128), 1)
    to2 = jnp.where(
        ((column < 40) & (src == column // 2)) | ((column >= 120) & (src == 64 + column // 2)), 1.0, 0.0
    )
    for x in range(6):
        rows[24 * x : 24 * x + 24] = source[2 * ix + x]
    rows[0:144] = dot(rows[0:144], to2)
    for x in range(6):
        duplicate(dup, 16 * x, rows, 24 * x + 10, 6)
        duplicate(dup, 16 * x + 12, rows, 24 * x + 8, 2)
        both = dup[16 * x : 16 * x + 16]
        a2[2 * x] = v2[2 * x] + both
        a2[2 * x + 1] = v2[2 * x + 1] + both
    sweep(1, 11, 10, k2, w2, g2, cy2, cz2, a2, b2)
    sweep(2, 10, 8, k2, w2, g2, cy2, cz2, b2, a2)

    to1 = jnp.where(
        ((column < 80) & (src == column // 2)) | ((column >= 112) & (src == 64 + column // 2)), 1.0, 0.0
    )
    for x in range(8):
        rows[16 * x : 16 * x + 16] = a2[x + 2]
    rows[0:128] = dot(rows[0:128], to1)
    for x in range(8):
        duplicate(dup, 24 * x, rows, 16 * x, 10)
        duplicate(dup, 24 * x + 20, rows, 16 * x + 14, 2)
        both = dup[24 * x : 24 * x + 24]
        a1[2 * x] = v1[2 * x] + both
        a1[2 * x + 1] = v1[2 * x + 1] + both
    sweep(2, 14, 12, k1, w1, g1, cy1, cz1, a1, b1)
    sweep(3, 13, 10, k1, w1, g1, cy1, cz1, b1, a1)

    to0 = jnp.where(iota((128, 256), 0) == iota((128, 256), 1) // 2, 1.0, 0.0)
    for x in range(10):
        rows[24 * x : 24 * x + 24] = a1[x + 3]
    wide[...] = dot(rows[0:240], to0)
    for x in range(10):
        for half, lanes in ((low, slice(0, 128)), (high, slice(128, 256))):
            mid = wide[24 * x : 24 * x + 18, lanes]
            half[pl.ds(0, 18, stride=2), :] = mid
            half[pl.ds(1, 18, stride=2), :] = mid
            ahead = wide[24 * x + 22 : 24 * x + 24, lanes]
            half[pl.ds(36, 2, stride=2), :] = ahead
            half[pl.ds(37, 2, stride=2), :] = ahead
            for p in (2 * x + 2, 2 * x + 3):
                a0[p, :, lanes] = v0[p, :, lanes] + half[...]
    sweep(3, 21, 3, k0, w0, g0, cy0, cz0, a0, b0)

    def values(p):
        total, centre = neighbours(p, k0, cy0, cz0, b0)
        return (KEEP * centre + g0[p] + w0[p] * total)[0:32, 0:128]

    def store(p, value):
        out[p - 4] = value

    planes(4, 20, values, store, 4)


VMEM = pl.BlockSpec(memory_space=pltpu.VMEM)
SMEM = pl.BlockSpec(memory_space=pltpu.SMEM)


COARSE_TARGETS = ((1, 3, 4, 5, 2, 7, 0, 6), (2, 7, 0, 1, 6, 3, 4, 5))


def call(kernel, outs, scratch, *args, pos=None):
    specs = [VMEM] * len(args)
    if pos is not None:
        args = (pos,) + args
        specs = [SMEM] + specs
    return pl.pallas_call(
        kernel,
        out_shape=[jax.ShapeDtypeStruct(s, F32) for s in outs],
        in_specs=specs,
        out_specs=[VMEM] * len(outs),
        scratch_shapes=[pltpu.VMEM(s, F32) for s in scratch],
        compiler_params=pltpu.CompilerParams(vmem_limit_bytes=16 * 1024 * 1024),
        name=getattr(kernel, "__name__", "pack_z1_kernel"),
    )(*args)


def shift(x, axis, step):
    size = lax.axis_size(axis)
    return lax.ppermute(x, axis, [(i, (i + step) % size) for i in range(size)])


def swap(x, axis, bits):
    size = lax.axis_size(axis)
    return lax.ppermute(x, axis, [(i, i ^ bits) for i in range(size)])


FULL, SIDES = (24, 40, 256), (2, 40, 128)
ONE, TWO, THREE = (40, 48, 128), (24, 24, 128), (12, 24, 128)
NEAR1, NEAR2 = (16, 24, 128), (12, 16, 128)
TALL = (768, 128)


def gather_x(x):
    return jnp.concatenate([x] + [swap(x, "gx", bits) for bits in (1, 2, 3)])


def both_sides(up, down, axis):
    return shift(up, axis, 1), shift(down, axis, -1)


def pack_z1(count, own, yl, yr):
    kernel = functools.partial(pack_z1_kernel, count)
    return call(kernel, [(4 * count, 48, 128)] * 2, [], own, yl, yr)


def per_device(f, k, m):
    pos = jnp.stack([lax.axis_index("gx"), lax.axis_index("gy"), lax.axis_index("gz")])
    pos = pos.astype(jnp.int32)
    xl = shift(jnp.concatenate([f[13:], m[13:], k[12:]]), "gx", 1)
    xr = shift(jnp.concatenate([f[:3], m[:3], k[:4]]), "gx", -1)

    (brick,) = call(coarse_kernel, [(8, 16, 128)], [(256, 128)], k, m)
    own = gather_x(brick)
    yl, yr = both_sides(own, own, "gy")
    zl, zr = both_sides(*pack_z1(2, own, yl, yr), "gz")
    coarsest, *static = call(
        static_kernel,
        [(2, 8, 128)] + [ONE] * 5 + [TWO] * 5 + [NEAR1] * 4 + [NEAR2] * 4,
        [ONE, TWO, TALL, (96, 128)],
        own, yl, yr, zl, zr,
        pos=pos,
    )
    whole, near = static[:10], static[10:]

    yl, yr = both_sides(*call(pack_y_kernel, [(240, 128)] * 2, [], f, k, m, xl, xr), "gy")
    fa, ka, ma, up, down = call(
        pack_z_kernel, [(24, 40, 128)] * 3 + [SIDES] * 2, [], f, k, m, xl, xr, yl, yr
    )
    zl, zr = both_sides(up, down, "gz")
    brick, *level0 = call(
        fine_kernel,
        [(4, 16, 128)] + [FULL] * 6,
        [FULL] * 3 + [(256, 128)],
        fa, ka, ma, zl, zr,
        pos=pos,
    )

    own = gather_x(brick)
    yl, yr = both_sides(own, own, "gy")
    zl, zr = both_sides(*pack_z1(1, own, yl, yr), "gz")
    message, *vary = call(
        middle_kernel,
        [(3, 8, 128)] + [NEAR1] * 2 + [NEAR2] * 2,
        [ONE] * 3 + [TWO] * 3 + [TALL, (96, 128)],
        own, yl, yr, zl, zr, coarsest, *whole,
        pos=pos,
    )

    own = jnp.concatenate([message, *both_sides(message, message, "gz")])
    first, second = (lax.ppermute(own, "gy", list(enumerate(t))) for t in COARSE_TARGETS)
    return call(
        last_kernel,
        [(16, 32, 128)],
        [THREE] * 9 + [(240, 128), (192, 128)] + [NEAR2] * 2 + [NEAR1] * 2
        + [(240, 256), (40, 128), (40, 128)] + [FULL] * 2,
        own, first, second, *level0, *vary, *near,
        pos=pos,
    )[0]


def solution(mesh):
    placed = (P("gx", "gy", "gz"), P("gx", "gy", "gz"), P("gx", "gy", "gz"))
    return jax.shard_map(
        per_device, mesh=mesh, in_specs=placed, out_specs=P("gx", "gy", "gz"), check_vma=False
    )
```

```python
import functools

import jax
import jax.numpy as jnp
from jax import lax
from jax.experimental import pallas as pl
from jax.experimental.pallas import tpu as pltpu
from jax.sharding import PartitionSpec as P

SWEEPS = 2
COARSE_SWEEPS = 8
OMEGA = 2.0 / 3.0
KEEP = 1.0 - OMEGA
OUTSIDE = 1e30
LIMIT = 1e29
F32 = jnp.float32
BF16 = jnp.bfloat16


def dot(a, b):
    high = a.astype(BF16)
    rest = a - high.astype(F32)
    middle = rest.astype(BF16)
    low = (rest - middle.astype(F32)).astype(BF16)
    terms = jnp.concatenate([high, middle, low], axis=1)
    matrix = b.astype(BF16)
    return jnp.dot(terms, jnp.concatenate([matrix] * 3, axis=0), preferred_element_type=F32)


def iota(shape, dim):
    return lax.broadcasted_iota(jnp.int32, shape, dim)


def roll(x, shift, axis):
    size = x.shape[axis]
    shift = shift % size
    return x if shift == 0 else pltpu.roll(x, shift, axis)


def after(x, axis):
    return roll(x, -1, axis)


def before(x, axis):
    return roll(x, 1, axis)


def planes(low, high, values, store, group):
    def run(first, count):
        found = [values(first + i) for i in range(count)]
        for i, value in enumerate(found):
            store(first + i, value)

    whole = (high - low) // group
    if whole == 1:
        run(low, group)
    elif whole:

        def step(index, carry):
            run(low + index * group, group)
            return carry

        lax.fori_loop(0, whole, step, 0)
    if (high - low) % group:
        run(low + whole * group, (high - low) % group)


def coefficients(low, high, group, k, f, m, d, w, g, cy, cz):
    def values(p):
        here = k[p]
        y = here + after(here, 0)
        z = here + after(here, 1)
        diagonal = m[p] + (k[p - 1] + here) + (here + k[p + 1])
        diagonal = diagonal + y + before(y, 0) + z + before(z, 1)
        weight = jnp.where(m[p] < LIMIT, OMEGA / diagonal, 0.0)
        return y, z, weight, diagonal, None if f is None else weight * f[p]

    def store(p, found):
        cy[p], cz[p], w[p] = found[:3]
        if d is not None:
            d[p] = found[3]
        if f is not None:
            g[p] = found[4]

    planes(low, high, values, store, group)


def neighbours(p, k, cy, cz, v):
    here, centre, y, z = k[p], v[p], cy[p], cz[p]
    total = (k[p - 1] + here) * v[p - 1] + (here + k[p + 1]) * v[p + 1]
    total = total + y * after(centre, 0) + before(y * centre, 0)
    total = total + z * after(centre, 1) + before(z * centre, 1)
    return total, centre


def sweep(low, high, group, k, w, g, cy, cz, v, out):
    def values(p):
        total, centre = neighbours(p, k, cy, cz, v)
        return KEEP * centre + g[p] + w[p] * total

    def store(p, value):
        out[p] = value

    planes(low, high, values, store, group)


def reach(p):
    away = max(0, 4 - p, p - 19)
    return max(0, 3 - away), 4 - away


def row_table():
    table, base = [], 0
    for p in range(24):
        three, four = reach(p)
        table.append((base, base + three, base + 2 * three))
        base += 2 * three + four
    return table, base


ROWS, ROW_COUNT = row_table()


def pack_y_kernel(f, k, m, xl, xr, up, down):
    for p in range(24):
        if p < 4:
            refs = ((xl, p - 1), (xl, 2 + p), (xl, 6 + p))
        elif p < 20:
            refs = ((f, p - 4), (m, p - 4), (k, p - 4))
        else:
            refs = ((xr, p - 20), (xr, p - 17), (xr, p - 14))
        for a, (ref, plane) in enumerate(refs):
            count, base = reach(p)[a // 2], ROWS[p][a]
            if count:
                up[base : base + count] = ref[plane, 32 - count : 32]
                down[base : base + count] = ref[plane, 0:count]


def pack_z_kernel(f, k, m, xl, xr, yl, yr, fa, ka, ma, up, down):
    lane = iota((40, 128), 1)
    zero = jnp.zeros((32, 128), F32)
    for g in range(2):
        acc_up = jnp.zeros((40, 128), F32)
        acc_down = jnp.zeros((40, 128), F32)
        for i in range(12):
            p = 12 * g + i
            if p < 4:
                own = (xl[p - 1] if p else zero, xl[2 + p] if p else zero, xl[6 + p])
            elif p < 20:
                own = (f[p - 4], m[p - 4], k[p - 4])
            else:
                own = (xr[p - 20] if p < 23 else zero, xr[p - 17] if p < 23 else zero, xr[p - 14])
            for a, out in enumerate((fa, ma, ka)):
                count, base = reach(p)[a // 2], ROWS[p][a]
                out[p, 0:32] = own[a]
                out[p, 32:40] = jnp.zeros((8, 128), F32)
                if count:
                    out[p, 32 : 32 + count] = yr[base : base + count]
                    out[p, 40 - count : 40] = yl[base : base + count]
                whole = out[p]
                width = 4 if a == 2 else 3
                first = 10 * i + 3 * a
                mask = (lane >= first) & (lane < first + width)
                acc_up = jnp.where(mask, roll(whole, first - (128 - width), 1), acc_up)
                acc_down = jnp.where(mask, roll(whole, first, 1), acc_down)
        up[g] = acc_up
        down[g] = acc_down


def pair_matrix(columns):
    return jnp.where(iota((128, columns), 0) // 2 == iota((128, columns), 1) % 64, 0.125, 0.0)


def coarse_kernel(k, m, message, tall):
    pairs = pair_matrix(128)
    for slot, ref in enumerate((m, k)):
        for i in range(8):
            tall[32 * i : 32 * i + 32] = ref[2 * i] + ref[2 * i + 1]
        halve_and_pack(tall, pairs, message, 4 * slot)


def halve_and_pack(tall, pairs, message, first):
    lane16 = iota((16, 128), 1)
    halves = tall[pl.ds(0, 128, stride=2), :] + tall[pl.ds(1, 128, stride=2), :]
    coarse = dot(halves, pairs)
    for i in range(4):
        message[first + i] = jnp.where(
            lane16 < 64, coarse[16 * i : 16 * i + 16], coarse[16 * i + 64 : 16 * i + 80]
        )


def fine_kernel(pos, fa, ka, ma, zl, zr, message, v_out, w, g, k, cy, cz, f, m, d, tall):
    ix, iy, iz = pos[0], pos[1], pos[2]
    row = iota((40, 128), 0)
    lane = iota((40, 128), 1)
    far = ((row >= 32) & (row < 36) & (iy == 7)) | ((row >= 36) & (iy == 0))
    beside = ((lane < 4) & (iz < 7)) | ((lane >= 124) & (iz > 0))
    inner = (lane < 3) | (lane > 124)
    for p in range(24):
        group, i = p // 12, p % 12
        absent = False
        if p < 4:
            absent = ix == 0
        elif p >= 20:
            absent = ix == 3
        gone = far | absent
        three = reach(p)[0]
        unknown = (row >= 32 + three) & (row < 40 - three)
        for a, (src, out) in enumerate(((fa, f), (ma, m), (ka, k))):
            width = 4 if a == 2 else 3
            first = 10 * i + 3 * a
            if a == 1 and p in (0, 23):
                out[p] = jnp.full((40, 256), OUTSIDE, F32)
                continue
            right = roll(zr[group], -first, 1)
            left = roll(zl[group], 128 - width - first, 1)
            side = jnp.where(lane < 64, right, left)
            own = src[p]
            fill = OUTSIDE if a == 1 else 0.0
            if a == 2:
                here, there = gone, gone | ~beside
                own, side = 0.5 * own, 0.5 * side
            else:
                here = gone | unknown
                there = here | ~(beside & inner)
            out[p, :, 0:128] = jnp.where(here, fill, own)
            out[p, :, 128:256] = jnp.where(there, fill, side)
    coefficients(1, 23, 4, k, f, m, d, w, g, cy, cz)
    sweep(2, 22, 4, k, w, g, cy, cz, g, v_out)

    def residual(p):
        total, centre = neighbours(p, k, cy, cz, v_out)
        return (f[p] + total - d[p] * centre)[0:32, 0:128]

    def values(i):
        return residual(2 * i + 4) + residual(2 * i + 5)

    def store(i, value):
        tall[pl.ds(pl.multiple_of(32 * i, 32), 32), :] = value

    planes(0, 8, values, store, 2)
    halve_and_pack(tall, pair_matrix(128), message, 0)


def pack_z1_kernel(count, own, yl, yr, up, down):
    lane = iota((16, 128), 1) % 64
    for b in range(4 * count):
        for part, src in enumerate((own, yr, yl)):
            acc_up = jnp.zeros((16, 128), F32)
            acc_down = jnp.zeros((16, 128), F32)
            for q in range(4):
                pair = src[4 * b + q]
                mask = (lane >= 16 * q) & (lane < 16 * q + 16)
                acc_up = jnp.where(mask, roll(pair, 16 * q - 48, 1), acc_up)
                acc_down = jnp.where(mask, roll(pair, 16 * q, 1), acc_down)
            up[b, 16 * part : 16 * part + 16] = acc_up
            down[b, 16 * part : 16 * part + 16] = acc_down


def clear(refs, low, high):
    for ref in refs:
        for p in (*range(low), *range(high, ref.shape[0])):
            ref[p] = jnp.zeros(ref.shape[1:], F32)


def outside1(iy, iz):
    row, lane = iota((48, 128), 0), iota((48, 128), 1)
    gone = ((row >= 16) & (row < 32) & (iy == 7)) | ((row >= 32) & (iy == 0))
    gone = gone | ((lane >= 64) & (lane < 80) & (iz == 7)) | ((lane >= 112) & (iz == 0))
    return gone | ((lane >= 80) & (lane < 112))


def spread1(ix, gone, own, yl, yr, zl, zr, order, count, a, out, fill, scale):
    lane = iota((48, 128), 1)
    for b in range(4):
        block = 8 * jnp.bitwise_xor(ix, order[b]) + 4
        left, right = zl[count * b + a], zr[count * b + a]
        for q in range(4):
            s = 4 * (count * b + a) + q
            pair = jnp.concatenate([own[s], yr[s], yl[s]], axis=0)
            for h in range(2):
                at = 16 * (q + 4 * h)
                side = jnp.where(lane < 96, roll(right, 64 - at, 1), roll(left, 112 - at, 1))
                value = jnp.where(lane < 64, roll(pair, 64 * h, 1), side)
                value = value if scale == 1.0 else scale * value
                out[block + q + 4 * h] = jnp.where(gone, fill, value)


def known2(shape):
    lane = iota(shape, 1)
    return (lane < 40) | (lane >= 120)


def to_second(tall, out, values, fill):
    def store(i, value):
        tall[pl.ds(pl.multiple_of(48 * i, 48), 48), :] = value

    planes(0, 16, lambda i: values(2 * i + 4) + values(2 * i + 5), store, 4)
    halves = tall[pl.ds(0, 384, stride=2), :] + tall[pl.ds(1, 384, stride=2), :]
    coarse = dot(halves, jnp.where(known2((128, 128)), pair_matrix(128), 0.0))
    for i in range(16):
        out[i + 4] = jnp.where(known2((24, 128)), coarse[24 * i : 24 * i + 24], fill)


def to_third(tall, small, write, values):
    for i in range(8):
        tall[24 * i : 24 * i + 24] = values(2 * i + 4) + values(2 * i + 5)
    halves = tall[pl.ds(0, 96, stride=2), :] + tall[pl.ds(1, 96, stride=2), :]
    spread = jnp.where(iota((128, 128), 0) // 2 == iota((128, 128), 1) % 16, 0.125, 0.0)
    small[0:96] = dot(halves, spread)
    group = iota((12, 128), 1) // 16
    packed = jnp.zeros((12, 128), F32)
    for i in range(8):
        packed = jnp.where(group == i, small[12 * i : 12 * i + 12], packed)
    small[0:12] = packed
    write(slice(0, 2), small[10:12])
    write(slice(2, 8), small[0:6])


def cut1(ix, src, out):
    for p in range(16):
        out[p, 0:20] = src[8 * ix + p, 0:20]
        out[p, 20:24] = src[8 * ix + p, 44:48]


def cut2(ix, src, out):
    for p in range(12):
        out[p, 0:12] = src[4 * ix + p, 0:12]
        out[p, 12:16] = src[4 * ix + p, 20:24]


def static_kernel(
    pos, own, yl, yr, zl, zr,
    coarsest, k1, w1, cy1, cz1, d1, k2, w2, cy2, cz2, d2,
    k1n, w1n, cy1n, cz1n, k2n, w2n, cy2n, cz2n,
    m1, m2, tall, small,
):
    ix, iy, iz = pos[0], pos[1], pos[2]
    gone = outside1(iy, iz)
    clear((k1, w1, cy1, cz1), 4, 36)
    clear((k2, w2, cy2, cz2), 4, 20)
    spread1(ix, gone, own, yl, yr, zl, zr, (0, 1, 2, 3), 2, 0, m1, OUTSIDE, 1.0)
    spread1(ix, gone, own, yl, yr, zl, zr, (0, 1, 2, 3), 2, 1, k1, 0.0, 0.125)
    coefficients(4, 36, 8, k1, None, m1, d1, w1, None, cy1, cz1)
    to_second(tall, m2, lambda p: m1[p], OUTSIDE)
    to_second(tall, k2, lambda p: 0.25 * k1[p], 0.0)
    coefficients(4, 20, 8, k2, None, m2, d2, w2, None, cy2, cz2)

    def write(slot):
        def put(where, value):
            coarsest[slot, where] = value

        return put

    to_third(tall, small, write(0), lambda p: m2[p])
    to_third(tall, small, write(1), lambda p: 0.25 * k2[p])
    for src, out in ((k1, k1n), (w1, w1n), (cy1, cy1n), (cz1, cz1n)):
        cut1(ix, src, out)
    for src, out in ((k2, k2n), (w2, w2n), (cy2, cy2n), (cz2, cz2n)):
        cut2(ix, src, out)


def middle_kernel(
    pos, own, yl, yr, zl, zr, coarsest, k1, w1, cy1, cz1, d1, k2, w2, cy2, cz2, d2,
    message, v1n, g1n, v2n, g2n,
    f1, g1, v1, f2, g2, v2, tall, small,
):
    ix, iy, iz = pos[0], pos[1], pos[2]
    gone = outside1(iy, iz)
    clear((g1, v1), 4, 36)
    clear((g2, v2), 4, 20)
    spread1(ix, gone, own, yl, yr, zl, zr, (0, 1, 2, 3), 1, 0, f1, 0.0, 1.0)

    def weigh(low, high, w, f, g):
        def store(p, value):
            g[p] = value

        planes(low, high, lambda p: w[p] * f[p], store, 8)

    weigh(4, 36, w1, f1, g1)
    sweep(4, 36, 8, k1, w1, g1, cy1, cz1, g1, v1)

    def residual1(p):
        total, centre = neighbours(p, k1, cy1, cz1, v1)
        return jnp.where(gone, 0.0, f1[p] + total - d1[p] * centre)

    to_second(tall, f2, residual1, 0.0)
    weigh(4, 20, w2, f2, g2)
    sweep(4, 20, 8, k2, w2, g2, cy2, cz2, g2, v2)
    row24 = iota((24, 128), 0)
    gone2 = ((row24 >= 8) & (row24 < 16) & (iy == 7)) | ((row24 >= 16) & (iy == 0))

    def residual2(p):
        total, centre = neighbours(p, k2, cy2, cz2, v2)
        return jnp.where(gone2, 0.0, f2[p] + total - d2[p] * centre)

    def put(where, value):
        message[0, where] = value

    to_third(tall, small, put, residual2)
    message[1] = coarsest[0]
    message[2] = coarsest[1]
    cut1(ix, v1, v1n)
    cut1(ix, g1, g1n)
    cut2(ix, v2, v2n)
    cut2(ix, g2, g2n)


def duplicate(out, base, rows, first, count):
    value = rows[first : first + count]
    out[pl.ds(base, count, stride=2), :] = value
    out[pl.ds(base + 1, count, stride=2), :] = value


def last_kernel(
    pos, own, first, second, v0, w0, g0, k0, cy0, cz0, v1, g1, v2, g2, k1, w1, cy1, cz1, k2, w2, cy2, cz2,
    out,
    k3, f3, m3, w3, g3, cy3, cz3, a3, b3, rows, dup, a2, b2, a1, b1, wide, low, high, a0, b0,
):
    ix, iy, iz = pos[0], pos[1], pos[2]
    row = iota((24, 128), 0) + 4 * iy - 10
    lane = iota((24, 128), 1)
    gone = (row < 0) | (row >= 32) | ((lane >= 32) & (lane < 112))
    gone = gone | ((lane >= 16) & (lane < 32) & (iz == 7)) | ((lane >= 112) & (iz == 0))
    clear((k3, g3, a3, b3), 2, 10)
    crossed = (iy // 2) % 2 == 0

    def stack(index):
        one, two = first[index], second[index]
        ahead, behind = jnp.where(crossed, two, one), jnp.where(crossed, one, two)
        ahead = jnp.where(iy == 1, roll(ahead, 4, 0), ahead)
        behind = jnp.where(iy == 6, roll(behind, 4, 0), behind)
        return jnp.concatenate([ahead, own[index], behind], axis=0)

    for a, (ref, fill) in enumerate(((f3, 0.0), (m3, OUTSIDE), (k3, 0.0))):
        here, left, right = (stack(3 * z + a) for z in range(3))
        for x in range(8):
            value = jnp.where(
                lane < 16,
                roll(here, -16 * x, 1),
                jnp.where(lane < 64, roll(right, 16 - 16 * x, 1), roll(left, 112 - 16 * x, 1)),
            )
            ref[x + 2] = jnp.where(gone, fill, value)
    coefficients(2, 10, 8, k3, f3, m3, None, w3, g3, cy3, cz3)
    source = g3
    for index in range(COARSE_SWEEPS - 1):
        target = (a3, b3)[index % 2]
        sweep(2, 10, 8, k3, w3, g3, cy3, cz3, source, target)
        source = target

    src, column = iota((128, 128), 0), iota((128, 128), 1)
    to2 = jnp.where(
        ((column < 40) & (src == column // 2)) | ((column >= 120) & (src == 64 + column // 2)), 1.0, 0.0
    )
    for x in range(6):
        rows[24 * x : 24 * x + 24] = source[2 * ix + x]
    rows[0:144] = dot(rows[0:144], to2)
    for x in range(6):
        duplicate(dup, 16 * x, rows, 24 * x + 10, 6)
        duplicate(dup, 16 * x + 12, rows, 24 * x + 8, 2)
        both = dup[16 * x : 16 * x + 16]
        a2[2 * x] = v2[2 * x] + both
        a2[2 * x + 1] = v2[2 * x + 1] + both
    sweep(1, 11, 10, k2, w2, g2, cy2, cz2, a2, b2)
    sweep(2, 10, 8, k2, w2, g2, cy2, cz2, b2, a2)

    to1 = jnp.where(
        ((column < 80) & (src == column // 2)) | ((column >= 112) & (src == 64 + column // 2)), 1.0, 0.0
    )
    for x in range(8):
        rows[16 * x : 16 * x + 16] = a2[x + 2]
    rows[0:128] = dot(rows[0:128], to1)
    for x in range(8):
        duplicate(dup, 24 * x, rows, 16 * x, 10)
        duplicate(dup, 24 * x + 20, rows, 16 * x + 14, 2)
        both = dup[24 * x : 24 * x + 24]
        a1[2 * x] = v1[2 * x] + both
        a1[2 * x + 1] = v1[2 * x + 1] + both
    sweep(2, 14, 12, k1, w1, g1, cy1, cz1, a1, b1)
    sweep(3, 13, 10, k1, w1, g1, cy1, cz1, b1, a1)

    to0 = jnp.where(iota((128, 256), 0) == iota((128, 256), 1) // 2, 1.0, 0.0)
    for x in range(10):
        rows[24 * x : 24 * x + 24] = a1[x + 3]
    wide[...] = dot(rows[0:240], to0)
    for x in range(10):
        for half, lanes in ((low, slice(0, 128)), (high, slice(128, 256))):
            mid = wide[24 * x : 24 * x + 18, lanes]
            half[pl.ds(0, 18, stride=2), :] = mid
            half[pl.ds(1, 18, stride=2), :] = mid
            ahead = wide[24 * x + 22 : 24 * x + 24, lanes]
            half[pl.ds(36, 2, stride=2), :] = ahead
            half[pl.ds(37, 2, stride=2), :] = ahead
            for p in (2 * x + 2, 2 * x + 3):
                a0[p, :, lanes] = v0[p, :, lanes] + half[...]
    sweep(3, 21, 3, k0, w0, g0, cy0, cz0, a0, b0)

    def values(p):
        total, centre = neighbours(p, k0, cy0, cz0, b0)
        return (KEEP * centre + g0[p] + w0[p] * total)[0:32, 0:128]

    def store(p, value):
        out[p - 4] = value

    planes(4, 20, values, store, 4)


VMEM = pl.BlockSpec(memory_space=pltpu.VMEM)
SMEM = pl.BlockSpec(memory_space=pltpu.SMEM)


COARSE_TARGETS = ((2, 3, 0, 1, 6, 7, 4, 5), (1, 0, 4, 5, 2, 3, 7, 6))


def call(kernel, outs, scratch, *args, pos=None):
    specs = [VMEM] * len(args)
    if pos is not None:
        args = (pos,) + args
        specs = [SMEM] + specs
    return pl.pallas_call(
        kernel,
        out_shape=[jax.ShapeDtypeStruct(s, F32) for s in outs],
        in_specs=specs,
        out_specs=[VMEM] * len(outs),
        scratch_shapes=[pltpu.VMEM(s, F32) for s in scratch],
        compiler_params=pltpu.CompilerParams(vmem_limit_bytes=16 * 1024 * 1024),
        name=getattr(kernel, "__name__", "pack_z1_kernel"),
    )(*args)


def shift(x, axis, step):
    size = lax.axis_size(axis)
    return lax.ppermute(x, axis, [(i, (i + step) % size) for i in range(size)])


def swap(x, axis, bits):
    size = lax.axis_size(axis)
    return lax.ppermute(x, axis, [(i, i ^ bits) for i in range(size)])


FULL, SIDES = (24, 40, 256), (2, 40, 128)
ONE, TWO, THREE = (40, 48, 128), (24, 24, 128), (12, 24, 128)
NEAR1, NEAR2 = (16, 24, 128), (12, 16, 128)
TALL = (768, 128)


def gather_x(x):
    return jnp.concatenate([x] + [swap(x, "gx", bits) for bits in (1, 2, 3)])


def gather_x_pairs(x):
    pair = jnp.concatenate([x, swap(x, "gx", 1)])
    return jnp.concatenate([pair, swap(pair, "gx", 3)])


def both_sides(up, down, axis):
    return shift(up, axis, 1), shift(down, axis, -1)


def pack_z1(count, own, yl, yr):
    kernel = functools.partial(pack_z1_kernel, count)
    return call(kernel, [(4 * count, 48, 128)] * 2, [], own, yl, yr)


def ordered(x, *others):
    return lax.optimization_barrier((x, *others))[0]


def per_device(f, k, m):
    pos = jnp.stack([lax.axis_index("gx"), lax.axis_index("gy"), lax.axis_index("gz")])
    pos = pos.astype(jnp.int32)

    up = jnp.concatenate([f[13:], m[13:], k[12:]])
    down = jnp.concatenate([f[:3], m[:3], k[:4]])
    xl, xr = both_sides(up, down, "gx")
    (brick,) = call(
        coarse_kernel, [(8, 16, 128)], [(256, 128)], k, m
    )
    static = gather_x(brick)

    yl, yr = both_sides(*call(pack_y_kernel, [(ROW_COUNT, 128)] * 2, [], f, k, m, xl, xr), "gy")
    fa, ka, ma, up, down = call(
        pack_z_kernel, [(24, 40, 128)] * 3 + [SIDES] * 2, [], f, k, m, xl, xr, yl, yr
    )
    zl, zr = both_sides(up, down, "gz")
    static_yl, static_yr = both_sides(static, static, "gy")
    brick, *level0 = call(
        fine_kernel,
        [(4, 16, 128)] + [FULL] * 6,
        [FULL] * 3 + [(256, 128)],
        fa, ka, ma, zl, zr,
        pos=pos,
    )
    static_up, static_down = pack_z1(2, static, static_yl, static_yr)

    own = gather_x(brick)
    static_zl, static_zr = both_sides(static_up, static_down, "gz")
    coarsest, *static = call(
        static_kernel,
        [(2, 8, 128)] + [ONE] * 5 + [TWO] * 5 + [NEAR1] * 4 + [NEAR2] * 4,
        [ONE, TWO, TALL, (96, 128)],
        static, static_yl, static_yr, static_zl, static_zr,
        pos=pos,
    )
    whole, near = static[:10], static[10:]
    yl, yr = both_sides(own, own, "gy")
    up, down = pack_z1(1, own, yl, yr)
    zl, zr = both_sides(up, down, "gz")
    message, *vary = call(
        middle_kernel,
        [(3, 8, 128)] + [NEAR1] * 2 + [NEAR2] * 2,
        [ONE] * 3 + [TWO] * 3 + [TALL, (96, 128)],
        own, yl, yr, zl, zr, coarsest, *whole,
        pos=pos,
    )

    own = jnp.concatenate([message, *both_sides(message, message, "gz")])
    first, second = (lax.ppermute(own, "gy", list(enumerate(t))) for t in COARSE_TARGETS)
    return call(
        last_kernel,
        [(16, 32, 128)],
        [THREE] * 9 + [(240, 128), (192, 128)] + [NEAR2] * 2 + [NEAR1] * 2
        + [(240, 256), (40, 128), (40, 128)] + [FULL] * 2,
        own, first, second, *level0, *vary, *near,
        pos=pos,
    )[0]


def solution(mesh):
    placed = (P("gx", "gy", "gz"), P("gx", "gy", "gz"), P("gx", "gy", "gz"))
    return jax.shard_map(
        per_device, mesh=mesh, in_specs=placed, out_specs=P("gx", "gy", "gz"), check_vma=False
    )
```

```python
import functools

import jax
import jax.numpy as jnp
from jax import lax
from jax.experimental import pallas as pl
from jax.experimental.pallas import tpu as pltpu
from jax.sharding import PartitionSpec as P

SWEEPS = 2
COARSE_SWEEPS = 8
OMEGA = 2.0 / 3.0
KEEP = 1.0 - OMEGA
OUTSIDE = 1e30
LIMIT = 1e29
F32 = jnp.float32
BF16 = jnp.bfloat16


def dot(a, b):
    high = a.astype(BF16)
    rest = a - high.astype(F32)
    middle = rest.astype(BF16)
    low = (rest - middle.astype(F32)).astype(BF16)
    terms = jnp.concatenate([high, middle, low], axis=1)
    matrix = b.astype(BF16)
    return jnp.dot(terms, jnp.concatenate([matrix] * 3, axis=0), preferred_element_type=F32)


def iota(shape, dim):
    return lax.broadcasted_iota(jnp.int32, shape, dim)


def roll(x, shift, axis):
    size = x.shape[axis]
    shift = shift % size
    return x if shift == 0 else pltpu.roll(x, shift, axis)


def after(x, axis):
    return roll(x, -1, axis)


def before(x, axis):
    return roll(x, 1, axis)


def planes(low, high, values, store, group):
    def run(first, count):
        found = [values(first + i) for i in range(count)]
        for i, value in enumerate(found):
            store(first + i, value)

    whole = (high - low) // group
    if whole == 1:
        run(low, group)
    elif whole:

        def step(index, carry):
            run(low + index * group, group)
            return carry

        lax.fori_loop(0, whole, step, 0)
    if (high - low) % group:
        run(low + whole * group, (high - low) % group)


def coefficients(low, high, group, k, f, m, d, w, g, cy, cz):
    def values(p):
        here = k[p]
        y = here + after(here, 0)
        z = here + after(here, 1)
        diagonal = m[p] + (k[p - 1] + here) + (here + k[p + 1])
        diagonal = diagonal + y + before(y, 0) + z + before(z, 1)
        weight = jnp.where(m[p] < LIMIT, OMEGA / diagonal, 0.0)
        return y, z, weight, diagonal, None if f is None else weight * f[p]

    def store(p, found):
        cy[p], cz[p], w[p] = found[:3]
        if d is not None:
            d[p] = found[3]
        if f is not None:
            g[p] = found[4]

    planes(low, high, values, store, group)


def neighbours(p, k, cy, cz, v):
    here, centre, y, z = k[p], v[p], cy[p], cz[p]
    total = (k[p - 1] + here) * v[p - 1] + (here + k[p + 1]) * v[p + 1]
    total = total + y * after(centre, 0) + before(y * centre, 0)
    total = total + z * after(centre, 1) + before(z * centre, 1)
    return total, centre


def sweep(low, high, group, k, w, g, cy, cz, v, out):
    def values(p):
        total, centre = neighbours(p, k, cy, cz, v)
        return KEEP * centre + g[p] + w[p] * total

    def store(p, value):
        out[p] = value

    planes(low, high, values, store, group)


def reach(p):
    away = max(0, 4 - p, p - 19)
    return max(0, 3 - away), 4 - away


def row_table():
    table, base = [], 0
    for p in range(24):
        three, four = reach(p)
        table.append((base, base + three, base + 2 * three))
        base += 2 * three + four
    return table, base


ROWS, ROW_COUNT = row_table()


def pack_y_kernel(f, k, m, xl, xr, up, down):
    for p in range(24):
        if p < 4:
            refs = ((xl, p - 1), (xl, 2 + p), (xl, 6 + p))
        elif p < 20:
            refs = ((f, p - 4), (m, p - 4), (k, p - 4))
        else:
            refs = ((xr, p - 20), (xr, p - 17), (xr, p - 14))
        for a, (ref, plane) in enumerate(refs):
            count, base = reach(p)[a // 2], ROWS[p][a]
            if count:
                up[base : base + count] = ref[plane, 32 - count : 32]
                down[base : base + count] = ref[plane, 0:count]


def pack_z_kernel(f, k, m, xl, xr, yl, yr, fa, ka, ma, up, down):
    lane = iota((40, 128), 1)
    zero = jnp.zeros((32, 128), F32)
    faces = [[None, None] for _ in range(3)]
    for p in range(24):
        g, i = p // 16, p % 16
        if p < 4:
            own = (xl[p - 1] if p else zero, xl[2 + p] if p else zero, xl[6 + p])
        elif p < 20:
            own = (f[p - 4], m[p - 4], k[p - 4])
        else:
            own = (xr[p - 20] if p < 23 else zero, xr[p - 17] if p < 23 else zero, xr[p - 14])
        for a, out in enumerate((fa, ma, ka)):
            count, base = reach(p)[a // 2], ROWS[p][a]
            out[p, 0:32] = own[a]
            out[p, 32:40] = jnp.zeros((8, 128), F32)
            if count:
                out[p, 32 : 32 + count] = yr[base : base + count]
                out[p, 40 - count : 40] = yl[base : base + count]
            moved = roll(out[p], 8 * i + 4, 1)
            faces[a][g] = moved if i == 0 else jnp.where(lane // 8 == i, moved, faces[a][g])
    front = lane % 8 < 4
    source, screening, conductivity = faces
    pairs = ((source[0], screening[0]), (source[1], screening[1]), conductivity)
    for g, (one, two) in enumerate(pairs):
        up[g] = jnp.where(front, one, roll(two, 4, 1))
        down[g] = jnp.where(front, roll(one, -4, 1), two)


def pair_matrix(columns):
    return jnp.where(iota((128, columns), 0) // 2 == iota((128, columns), 1) % 64, 0.125, 0.0)


def coarse_kernel(k, m, message, tall):
    pairs = pair_matrix(128)
    for slot, ref in enumerate((m, k)):
        for i in range(8):
            tall[32 * i : 32 * i + 32] = ref[2 * i] + ref[2 * i + 1]
        halve_and_pack(tall, pairs, message, 4 * slot)


def halve_and_pack(tall, pairs, message, first):
    lane16 = iota((16, 128), 1)
    halves = tall[pl.ds(0, 128, stride=2), :] + tall[pl.ds(1, 128, stride=2), :]
    coarse = dot(halves, pairs)
    for i in range(4):
        message[first + i] = jnp.where(
            lane16 < 64, coarse[16 * i : 16 * i + 16], coarse[16 * i + 64 : 16 * i + 80]
        )


def fine_kernel(pos, fa, ka, ma, zl, zr, message, v_out, w, g, k, cy, cz, f, m, d, tall):
    ix, iy, iz = pos[0], pos[1], pos[2]
    row = iota((40, 128), 0)
    lane = iota((40, 128), 1)
    far = ((row >= 32) & (row < 36) & (iy == 7)) | ((row >= 36) & (iy == 0))
    beside = ((lane < 4) & (iz < 7)) | ((lane >= 124) & (iz > 0))
    inner = (lane < 3) | (lane > 124)
    front = lane % 8 < 4
    ones = [jnp.where(front, zl[g], roll(zr[g], 4, 1)) for g in range(3)]
    twos = [jnp.where(front, roll(zl[g], -4, 1), zr[g]) for g in range(3)]
    faces = (ones[:2], twos[:2], (ones[2], twos[2]))
    for p in range(24):
        group, i = p // 16, p % 16
        absent = False
        if p < 4:
            absent = ix == 0
        elif p >= 20:
            absent = ix == 3
        gone = far | absent
        three = reach(p)[0]
        unknown = (row >= 32 + three) & (row < 40 - three)
        for a, (src, out) in enumerate(((fa, f), (ma, m), (ka, k))):
            if a == 1 and p in (0, 23):
                out[p] = jnp.full((40, 256), OUTSIDE, F32)
                continue
            side = roll(faces[a][group], -8 * i - 4, 1)
            own = src[p]
            fill = OUTSIDE if a == 1 else 0.0
            if a == 2:
                here, there = gone, gone | ~beside
                own, side = 0.5 * own, 0.5 * side
            else:
                here = gone | unknown
                there = here | ~(beside & inner)
            out[p, :, 0:128] = jnp.where(here, fill, own)
            out[p, :, 128:256] = jnp.where(there, fill, side)
    coefficients(1, 23, 11, k, f, m, d, w, g, cy, cz)
    sweep(2, 22, 10, k, w, g, cy, cz, g, v_out)

    def residual(p):
        total, centre = neighbours(p, k, cy, cz, v_out)
        return (f[p] + total - d[p] * centre)[0:32, 0:128]

    def values(i):
        return residual(2 * i + 4) + residual(2 * i + 5)

    def store(i, value):
        tall[pl.ds(pl.multiple_of(32 * i, 32), 32), :] = value

    planes(0, 8, values, store, 8)
    halve_and_pack(tall, pair_matrix(128), message, 0)


def pack_z1_kernel(count, own, yl, yr, up, down):
    lane = iota((16, 128), 1) % 64
    for b in range(4 * count):
        for part, src in enumerate((own, yr, yl)):
            acc_up = jnp.zeros((16, 128), F32)
            acc_down = jnp.zeros((16, 128), F32)
            for q in range(4):
                pair = src[4 * b + q]
                mask = (lane >= 16 * q) & (lane < 16 * q + 16)
                acc_up = jnp.where(mask, roll(pair, 16 * q - 48, 1), acc_up)
                acc_down = jnp.where(mask, roll(pair, 16 * q, 1), acc_down)
            up[b, 16 * part : 16 * part + 16] = acc_up
            down[b, 16 * part : 16 * part + 16] = acc_down


def clear(refs, low, high):
    for ref in refs:
        for p in (*range(low), *range(high, ref.shape[0])):
            ref[p] = jnp.zeros(ref.shape[1:], F32)


def outside1(iy, iz):
    row, lane = iota((48, 128), 0), iota((48, 128), 1)
    gone = ((row >= 16) & (row < 32) & (iy == 7)) | ((row >= 32) & (iy == 0))
    gone = gone | ((lane >= 64) & (lane < 80) & (iz == 7)) | ((lane >= 112) & (iz == 0))
    return gone | ((lane >= 80) & (lane < 112))


def spread1(ix, gone, own, yl, yr, zl, zr, order, count, a, out, fill, scale):
    lane = iota((48, 128), 1)
    even = lane // 16 % 2 == 0
    for b in range(4):
        block = 8 * jnp.bitwise_xor(ix, order[b]) + 4
        left, right = roll(zl[count * b + a], 48, 1), zr[count * b + a]
        sides = (jnp.where(even, right, left), jnp.where(even, left, right))
        for q in range(4):
            s = 4 * (count * b + a) + q
            pair = jnp.concatenate([own[s], yr[s], yl[s]], axis=0)
            for h in range(2):
                at = 16 * (q + 4 * h)
                side = roll(sides[q % 2], 64 - at, 1)
                value = jnp.where(lane < 64, roll(pair, 64 * h, 1), side)
                value = value if scale == 1.0 else scale * value
                out[block + q + 4 * h] = jnp.where(gone, fill, value)


def known2(shape):
    lane = iota(shape, 1)
    return (lane < 40) | (lane >= 120)


def to_second(tall, out, values, fill):
    def store(i, value):
        tall[pl.ds(pl.multiple_of(48 * i, 48), 48), :] = value

    planes(0, 16, lambda i: values(2 * i + 4) + values(2 * i + 5), store, 4)
    halves = tall[pl.ds(0, 384, stride=2), :] + tall[pl.ds(1, 384, stride=2), :]
    coarse = dot(halves, jnp.where(known2((128, 128)), pair_matrix(128), 0.0))
    for i in range(16):
        out[i + 4] = jnp.where(known2((24, 128)), coarse[24 * i : 24 * i + 24], fill)


def to_third(tall, small, write, values):
    for i in range(8):
        tall[24 * i : 24 * i + 24] = values(2 * i + 4) + values(2 * i + 5)
    halves = tall[pl.ds(0, 96, stride=2), :] + tall[pl.ds(1, 96, stride=2), :]
    spread = jnp.where(iota((128, 128), 0) // 2 == iota((128, 128), 1) % 16, 0.125, 0.0)
    small[0:96] = dot(halves, spread)
    group = iota((12, 128), 1) // 16
    packed = jnp.zeros((12, 128), F32)
    for i in range(8):
        packed = jnp.where(group == i, small[12 * i : 12 * i + 12], packed)
    small[0:12] = packed
    write(slice(0, 2), small[10:12])
    write(slice(2, 8), small[0:6])


def cut1(ix, src, out):
    for p in range(16):
        out[p, 0:20] = src[8 * ix + p, 0:20]
        out[p, 20:24] = src[8 * ix + p, 44:48]


def cut2(ix, src, out):
    for p in range(12):
        out[p, 0:12] = src[4 * ix + p, 0:12]
        out[p, 12:16] = src[4 * ix + p, 20:24]


def static_kernel(
    pos, own, yl, yr, zl, zr,
    coarsest, k1, w1, cy1, cz1, d1, k2, w2, cy2, cz2, d2,
    k1n, w1n, cy1n, cz1n, k2n, w2n, cy2n, cz2n,
    m1, m2, tall, small,
):
    ix, iy, iz = pos[0], pos[1], pos[2]
    gone = outside1(iy, iz)
    clear((k1, w1, cy1, cz1), 4, 36)
    clear((k2, w2, cy2, cz2), 4, 20)
    spread1(ix, gone, own, yl, yr, zl, zr, (0, 1, 2, 3), 2, 0, m1, OUTSIDE, 1.0)
    spread1(ix, gone, own, yl, yr, zl, zr, (0, 1, 2, 3), 2, 1, k1, 0.0, 0.125)
    coefficients(4, 36, 8, k1, None, m1, d1, w1, None, cy1, cz1)
    to_second(tall, m2, lambda p: m1[p], OUTSIDE)
    to_second(tall, k2, lambda p: 0.25 * k1[p], 0.0)
    coefficients(4, 20, 16, k2, None, m2, d2, w2, None, cy2, cz2)

    def write(slot):
        def put(where, value):
            coarsest[slot, where] = value

        return put

    to_third(tall, small, write(0), lambda p: m2[p])
    to_third(tall, small, write(1), lambda p: 0.25 * k2[p])
    for src, out in ((k1, k1n), (w1, w1n), (cy1, cy1n), (cz1, cz1n)):
        cut1(ix, src, out)
    for src, out in ((k2, k2n), (w2, w2n), (cy2, cy2n), (cz2, cz2n)):
        cut2(ix, src, out)


def middle_kernel(
    pos, own, yl, yr, zl, zr, coarsest, k1, w1, cy1, cz1, d1, k2, w2, cy2, cz2, d2,
    message, v1n, g1n, v2n, g2n,
    f1, g1, v1, f2, g2, v2, tall, small,
):
    ix, iy, iz = pos[0], pos[1], pos[2]
    gone = outside1(iy, iz)
    clear((g1, v1), 4, 36)
    clear((g2, v2), 4, 20)
    spread1(ix, gone, own, yl, yr, zl, zr, (0, 1, 2, 3), 1, 0, f1, 0.0, 1.0)

    def weigh(low, high, w, f, g):
        def store(p, value):
            g[p] = value

        planes(low, high, lambda p: w[p] * f[p], store, 8)

    weigh(4, 36, w1, f1, g1)
    sweep(4, 36, 16, k1, w1, g1, cy1, cz1, g1, v1)

    def residual1(p):
        total, centre = neighbours(p, k1, cy1, cz1, v1)
        return jnp.where(gone, 0.0, f1[p] + total - d1[p] * centre)

    to_second(tall, f2, residual1, 0.0)
    weigh(4, 20, w2, f2, g2)
    sweep(4, 20, 16, k2, w2, g2, cy2, cz2, g2, v2)
    row24 = iota((24, 128), 0)
    gone2 = ((row24 >= 8) & (row24 < 16) & (iy == 7)) | ((row24 >= 16) & (iy == 0))

    def residual2(p):
        total, centre = neighbours(p, k2, cy2, cz2, v2)
        return jnp.where(gone2, 0.0, f2[p] + total - d2[p] * centre)

    def put(where, value):
        message[0, where] = value

    to_third(tall, small, put, residual2)
    message[1] = coarsest[0]
    message[2] = coarsest[1]
    cut1(ix, v1, v1n)
    cut1(ix, g1, g1n)
    cut2(ix, v2, v2n)
    cut2(ix, g2, g2n)


def duplicate(out, base, rows, first, count):
    value = rows[first : first + count]
    out[pl.ds(base, count, stride=2), :] = value
    out[pl.ds(base + 1, count, stride=2), :] = value


def last_kernel(
    pos, own, first, second, v0, w0, g0, k0, cy0, cz0, v1, g1, v2, g2, k1, w1, cy1, cz1, k2, w2, cy2, cz2,
    out,
    k3, f3, m3, w3, g3, cy3, cz3, a3, b3, rows, dup, a2, b2, a1, b1, wide, low, high, a0, b0,
):
    ix, iy, iz = pos[0], pos[1], pos[2]
    row = iota((24, 128), 0) + 4 * iy - 10
    lane = iota((24, 128), 1)
    gone = (row < 0) | (row >= 32) | ((lane >= 32) & (lane < 112))
    gone = gone | ((lane >= 16) & (lane < 32) & (iz == 7)) | ((lane >= 112) & (iz == 0))
    clear((k3, g3, a3, b3), 2, 10)
    crossed = (iy // 2) % 2 == 0

    def stack(index):
        one, two = first[index], second[index]
        ahead, behind = jnp.where(crossed, two, one), jnp.where(crossed, one, two)
        ahead = jnp.where(iy == 1, roll(ahead, 4, 0), ahead)
        behind = jnp.where(iy == 6, roll(behind, 4, 0), behind)
        return jnp.concatenate([ahead, own[index], behind], axis=0)

    for a, (ref, fill) in enumerate(((f3, 0.0), (m3, OUTSIDE), (k3, 0.0))):
        here, left, right = (stack(3 * z + a) for z in range(3))
        for x in range(8):
            value = jnp.where(
                lane < 16,
                roll(here, -16 * x, 1),
                jnp.where(lane < 64, roll(right, 16 - 16 * x, 1), roll(left, 112 - 16 * x, 1)),
            )
            ref[x + 2] = jnp.where(gone, fill, value)
    coefficients(2, 10, 8, k3, f3, m3, None, w3, g3, cy3, cz3)
    source = g3
    for index in range(COARSE_SWEEPS - 1):
        target = (a3, b3)[index % 2]
        sweep(2, 10, 8, k3, w3, g3, cy3, cz3, source, target)
        source = target

    src, column = iota((128, 128), 0), iota((128, 128), 1)
    to2 = jnp.where(
        ((column < 40) & (src == column // 2)) | ((column >= 120) & (src == 64 + column // 2)), 1.0, 0.0
    )
    for x in range(6):
        rows[24 * x : 24 * x + 24] = source[2 * ix + x]
    rows[0:144] = dot(rows[0:144], to2)
    for x in range(6):
        duplicate(dup, 16 * x, rows, 24 * x + 10, 6)
        duplicate(dup, 16 * x + 12, rows, 24 * x + 8, 2)
        both = dup[16 * x : 16 * x + 16]
        a2[2 * x] = v2[2 * x] + both
        a2[2 * x + 1] = v2[2 * x + 1] + both
    sweep(1, 11, 10, k2, w2, g2, cy2, cz2, a2, b2)
    sweep(2, 10, 8, k2, w2, g2, cy2, cz2, b2, a2)

    to1 = jnp.where(
        ((column < 80) & (src == column // 2)) | ((column >= 112) & (src == 64 + column // 2)), 1.0, 0.0
    )
    for x in range(8):
        rows[16 * x : 16 * x + 16] = a2[x + 2]
    rows[0:128] = dot(rows[0:128], to1)
    for x in range(8):
        duplicate(dup, 24 * x, rows, 16 * x, 10)
        duplicate(dup, 24 * x + 20, rows, 16 * x + 14, 2)
        both = dup[24 * x : 24 * x + 24]
        a1[2 * x] = v1[2 * x] + both
        a1[2 * x + 1] = v1[2 * x + 1] + both
    sweep(2, 14, 12, k1, w1, g1, cy1, cz1, a1, b1)
    sweep(3, 13, 10, k1, w1, g1, cy1, cz1, b1, a1)

    to0 = jnp.where(iota((128, 256), 0) == iota((128, 256), 1) // 2, 1.0, 0.0)
    for x in range(10):
        rows[24 * x : 24 * x + 24] = a1[x + 3]
    wide[...] = dot(rows[0:240], to0)
    for x in range(10):
        for half, lanes in ((low, slice(0, 128)), (high, slice(128, 256))):
            mid = wide[24 * x : 24 * x + 18, lanes]
            half[pl.ds(0, 18, stride=2), :] = mid
            half[pl.ds(1, 18, stride=2), :] = mid
            ahead = wide[24 * x + 22 : 24 * x + 24, lanes]
            half[pl.ds(36, 2, stride=2), :] = ahead
            half[pl.ds(37, 2, stride=2), :] = ahead
            for p in (2 * x + 2, 2 * x + 3):
                a0[p, :, lanes] = v0[p, :, lanes] + half[...]
    sweep(3, 21, 9, k0, w0, g0, cy0, cz0, a0, b0)

    def values(p):
        total, centre = neighbours(p, k0, cy0, cz0, b0)
        return (KEEP * centre + g0[p] + w0[p] * total)[0:32, 0:128]

    def store(p, value):
        out[p - 4] = value

    planes(4, 20, values, store, 8)


VMEM = pl.BlockSpec(memory_space=pltpu.VMEM)
SMEM = pl.BlockSpec(memory_space=pltpu.SMEM)


COARSE_TARGETS = ((2, 3, 0, 1, 6, 7, 4, 5), (1, 0, 4, 5, 2, 3, 7, 6))


def call(kernel, outs, scratch, *args, pos=None):
    specs = [VMEM] * len(args)
    if pos is not None:
        args = (pos,) + args
        specs = [SMEM] + specs
    return pl.pallas_call(
        kernel,
        out_shape=[jax.ShapeDtypeStruct(s, F32) for s in outs],
        in_specs=specs,
        out_specs=[VMEM] * len(outs),
        scratch_shapes=[pltpu.VMEM(s, F32) for s in scratch],
        compiler_params=pltpu.CompilerParams(vmem_limit_bytes=16 * 1024 * 1024),
        name=getattr(kernel, "__name__", "pack_z1_kernel"),
    )(*args)


def shift(x, axis, step):
    size = lax.axis_size(axis)
    return lax.ppermute(x, axis, [(i, (i + step) % size) for i in range(size)])


def swap(x, axis, bits):
    size = lax.axis_size(axis)
    return lax.ppermute(x, axis, [(i, i ^ bits) for i in range(size)])


FULL, SIDES = (24, 40, 256), (3, 40, 128)
ONE, TWO, THREE = (40, 48, 128), (24, 24, 128), (12, 24, 128)
NEAR1, NEAR2 = (16, 24, 128), (12, 16, 128)
TALL = (768, 128)


def gather_x(x):
    return jnp.concatenate([x] + [swap(x, "gx", bits) for bits in (1, 2, 3)])


def gather_x_pairs(x):
    pair = jnp.concatenate([x, swap(x, "gx", 1)])
    return jnp.concatenate([pair, swap(pair, "gx", 3)])


def both_sides(up, down, axis):
    return shift(up, axis, 1), shift(down, axis, -1)


def pack_z1(count, own, yl, yr):
    kernel = functools.partial(pack_z1_kernel, count)
    return call(kernel, [(4 * count, 48, 128)] * 2, [], own, yl, yr)


def ordered(x, *others):
    return lax.optimization_barrier((x, *others))[0]


def per_device(f, k, m):
    pos = jnp.stack([lax.axis_index("gx"), lax.axis_index("gy"), lax.axis_index("gz")])
    pos = pos.astype(jnp.int32)

    up = jnp.concatenate([f[13:], m[13:], k[12:]])
    down = jnp.concatenate([f[:3], m[:3], k[:4]])
    xl, xr = both_sides(up, down, "gx")
    (brick,) = call(
        coarse_kernel, [(8, 16, 128)], [(256, 128)], k, m
    )
    static = gather_x(brick)

    yl, yr = both_sides(*call(pack_y_kernel, [(ROW_COUNT, 128)] * 2, [], f, k, m, xl, xr), "gy")
    fa, ka, ma, up, down = call(
        pack_z_kernel, [(24, 40, 128)] * 3 + [SIDES] * 2, [], f, k, m, xl, xr, yl, yr
    )
    zl, zr = both_sides(up, down, "gz")
    static_yl, static_yr = both_sides(static, static, "gy")
    brick, *level0 = call(
        fine_kernel,
        [(4, 16, 128)] + [FULL] * 6,
        [FULL] * 3 + [(256, 128)],
        fa, ka, ma, zl, zr,
        pos=pos,
    )
    static_up, static_down = pack_z1(2, static, static_yl, static_yr)

    own = gather_x(brick)
    static_zl, static_zr = both_sides(static_up, static_down, "gz")
    coarsest, *static = call(
        static_kernel,
        [(2, 8, 128)] + [ONE] * 5 + [TWO] * 5 + [NEAR1] * 4 + [NEAR2] * 4,
        [ONE, TWO, TALL, (96, 128)],
        static, static_yl, static_yr, static_zl, static_zr,
        pos=pos,
    )
    whole, near = static[:10], static[10:]
    yl, yr = both_sides(own, own, "gy")
    up, down = pack_z1(1, own, yl, yr)
    zl, zr = both_sides(up, down, "gz")
    message, *vary = call(
        middle_kernel,
        [(3, 8, 128)] + [NEAR1] * 2 + [NEAR2] * 2,
        [ONE] * 3 + [TWO] * 3 + [TALL, (96, 128)],
        own, yl, yr, zl, zr, coarsest, *whole,
        pos=pos,
    )

    own = jnp.concatenate([message, *both_sides(message, message, "gz")])
    first, second = (lax.ppermute(own, "gy", list(enumerate(t))) for t in COARSE_TARGETS)
    return call(
        last_kernel,
        [(16, 32, 128)],
        [THREE] * 9 + [(240, 128), (192, 128)] + [NEAR2] * 2 + [NEAR1] * 2
        + [(240, 256), (40, 128), (40, 128)] + [FULL] * 2,
        own, first, second, *level0, *vary, *near,
        pos=pos,
    )[0]


def solution(mesh):
    placed = (P("gx", "gy", "gz"), P("gx", "gy", "gz"), P("gx", "gy", "gz"))
    return jax.shard_map(
        per_device, mesh=mesh, in_specs=placed, out_specs=P("gx", "gy", "gz"), check_vma=False
    )
```

```python
import functools

import jax
import jax.numpy as jnp
from jax import lax
from jax.experimental import pallas as pl
from jax.experimental.pallas import tpu as pltpu
from jax.sharding import PartitionSpec as P

SWEEPS = 2
COARSE_SWEEPS = 8
OMEGA = 2.0 / 3.0
KEEP = 1.0 - OMEGA
OUTSIDE = 1e30
LIMIT = 1e29
F32 = jnp.float32
BF16 = jnp.bfloat16


def dot(a, b):
    high = a.astype(BF16)
    rest = a - high.astype(F32)
    middle = rest.astype(BF16)
    low = (rest - middle.astype(F32)).astype(BF16)
    terms = jnp.concatenate([high, middle, low], axis=1)
    matrix = b.astype(BF16)
    return jnp.dot(terms, jnp.concatenate([matrix] * 3, axis=0), preferred_element_type=F32)


def iota(shape, dim):
    return lax.broadcasted_iota(jnp.int32, shape, dim)


def roll(x, shift, axis):
    size = x.shape[axis]
    shift = shift % size
    return x if shift == 0 else pltpu.roll(x, shift, axis)


def after(x, axis):
    return roll(x, -1, axis)


def before(x, axis):
    return roll(x, 1, axis)


def planes(low, high, values, store, group):
    def run(first, count):
        found = [values(first + i) for i in range(count)]
        for i, value in enumerate(found):
            store(first + i, value)

    whole = (high - low) // group
    if whole == 1:
        run(low, group)
    elif whole:

        def step(index, carry):
            run(low + index * group, group)
            return carry

        lax.fori_loop(0, whole, step, 0)
    if (high - low) % group:
        run(low + whole * group, (high - low) % group)


def coefficients(low, high, group, k, f, m, d, w, g, cy, cz):
    def values(p):
        here = k[p]
        y = here + after(here, 0)
        z = here + after(here, 1)
        diagonal = m[p] + (k[p - 1] + here) + (here + k[p + 1])
        diagonal = diagonal + y + before(y, 0) + z + before(z, 1)
        weight = jnp.where(m[p] < LIMIT, OMEGA / diagonal, 0.0)
        return y, z, weight, diagonal, None if f is None else weight * f[p]

    def store(p, found):
        cy[p], cz[p], w[p] = found[:3]
        if d is not None:
            d[p] = found[3]
        if f is not None:
            g[p] = found[4]

    planes(low, high, values, store, group)


def neighbours(p, k, cy, cz, v):
    here, centre, y, z = k[p], v[p], cy[p], cz[p]
    total = (k[p - 1] + here) * v[p - 1] + (here + k[p + 1]) * v[p + 1]
    total = total + y * after(centre, 0) + before(y * centre, 0)
    total = total + z * after(centre, 1) + before(z * centre, 1)
    return total, centre


def sweep(low, high, group, k, w, g, cy, cz, v, out):
    def values(p):
        total, centre = neighbours(p, k, cy, cz, v)
        return KEEP * centre + g[p] + w[p] * total

    def store(p, value):
        out[p] = value

    planes(low, high, values, store, group)


def reach(p):
    away = max(0, 4 - p, p - 19)
    return max(0, 3 - away), 4 - away


def row_table():
    table, base = [], 0
    for p in range(24):
        three, four = reach(p)
        table.append((base, base + three, base + 2 * three))
        base += 2 * three + four
    return table, base


ROWS, ROW_COUNT = row_table()


def pack_y_kernel(f, k, m, xl, xr, up, down):
    for p in range(24):
        if p < 4:
            refs = ((xl, p - 1), (xl, 2 + p), (xl, 6 + p))
        elif p < 20:
            refs = ((f, p - 4), (m, p - 4), (k, p - 4))
        else:
            refs = ((xr, p - 20), (xr, p - 17), (xr, p - 14))
        for a, (ref, plane) in enumerate(refs):
            count, base = reach(p)[a // 2], ROWS[p][a]
            if count:
                up[base : base + count] = ref[plane, 32 - count : 32]
                down[base : base + count] = ref[plane, 0:count]


def pack_z_kernel(f, k, m, xl, xr, yl, yr, fa, ka, ma, up, down):
    lane = iota((40, 128), 1)
    zero = jnp.zeros((32, 128), F32)
    faces = [[None, None] for _ in range(3)]
    for p in range(24):
        g, i = p // 16, p % 16
        if p < 4:
            own = (xl[p - 1] if p else zero, xl[2 + p] if p else zero, xl[6 + p])
        elif p < 20:
            own = (f[p - 4], m[p - 4], k[p - 4])
        else:
            own = (xr[p - 20] if p < 23 else zero, xr[p - 17] if p < 23 else zero, xr[p - 14])
        for a, out in enumerate((fa, ma, ka)):
            count, base = reach(p)[a // 2], ROWS[p][a]
            out[p, 0:32] = own[a]
            out[p, 32:40] = jnp.zeros((8, 128), F32)
            if count:
                out[p, 32 : 32 + count] = yr[base : base + count]
                out[p, 40 - count : 40] = yl[base : base + count]
            moved = roll(out[p], 8 * i + 4, 1)
            faces[a][g] = moved if i == 0 else jnp.where(lane // 8 == i, moved, faces[a][g])
    front = lane % 8 < 4
    source, screening, conductivity = faces
    pairs = ((source[0], screening[0]), (source[1], screening[1]), conductivity)
    for g, (one, two) in enumerate(pairs):
        up[g] = jnp.where(front, one, roll(two, 4, 1))
        down[g] = jnp.where(front, roll(one, -4, 1), two)


def pair_matrix(columns):
    return jnp.where(iota((128, columns), 0) // 2 == iota((128, columns), 1) % 64, 0.125, 0.0)


def coarse_kernel(k, m, message, tall):
    pairs = pair_matrix(128)
    for slot, ref in enumerate((m, k)):
        for i in range(8):
            tall[32 * i : 32 * i + 32] = ref[2 * i] + ref[2 * i + 1]
        halve_and_pack(tall, pairs, message, 4 * slot)


def halve_and_pack(tall, pairs, message, first):
    lane16 = iota((16, 128), 1)
    halves = tall[pl.ds(0, 128, stride=2), :] + tall[pl.ds(1, 128, stride=2), :]
    coarse = dot(halves, pairs)
    for i in range(4):
        message[first + i] = jnp.where(
            lane16 < 64, coarse[16 * i : 16 * i + 16], coarse[16 * i + 64 : 16 * i + 80]
        )


def fine_kernel(pos, fa, ka, ma, zl, zr, message, v_out, w, g, k, cy, cz, f, m, d, tall):
    ix, iy, iz = pos[0], pos[1], pos[2]
    row = iota((40, 128), 0)
    lane = iota((40, 128), 1)
    far = ((row >= 32) & (row < 36) & (iy == 7)) | ((row >= 36) & (iy == 0))
    beside = ((lane < 4) & (iz < 7)) | ((lane >= 124) & (iz > 0))
    inner = (lane < 3) | (lane > 124)
    front = lane % 8 < 4
    ones = [jnp.where(front, zl[g], roll(zr[g], 4, 1)) for g in range(3)]
    twos = [jnp.where(front, roll(zl[g], -4, 1), zr[g]) for g in range(3)]
    faces = (ones[:2], twos[:2], (ones[2], twos[2]))
    for p in range(24):
        group, i = p // 16, p % 16
        absent = False
        if p < 4:
            absent = ix == 0
        elif p >= 20:
            absent = ix == 3
        gone = far | absent
        three = reach(p)[0]
        unknown = (row >= 32 + three) & (row < 40 - three)
        for a, (src, out) in enumerate(((fa, f), (ma, m), (ka, k))):
            if a == 1 and p in (0, 23):
                out[p] = jnp.full((40, 256), OUTSIDE, F32)
                continue
            side = roll(faces[a][group], -8 * i - 4, 1)
            own = src[p]
            fill = OUTSIDE if a == 1 else 0.0
            if a == 2:
                here, there = gone, gone | ~beside
                own, side = 0.5 * own, 0.5 * side
            else:
                here = gone | unknown
                there = here | ~(beside & inner)
            out[p, :, 0:128] = jnp.where(here, fill, own)
            out[p, :, 128:256] = jnp.where(there, fill, side)
    coefficients(1, 23, 11, k, f, m, d, w, g, cy, cz)
    sweep(2, 22, 10, k, w, g, cy, cz, g, v_out)

    def residual(p):
        total, centre = neighbours(p, k, cy, cz, v_out)
        return (f[p] + total - d[p] * centre)[0:32, 0:128]

    def values(i):
        return residual(2 * i + 4) + residual(2 * i + 5)

    def store(i, value):
        tall[pl.ds(pl.multiple_of(32 * i, 32), 32), :] = value

    planes(0, 8, values, store, 8)
    halve_and_pack(tall, pair_matrix(128), message, 0)


def pack_z1_kernel(count, own, yl, yr, up, down):
    lane = iota((16, 128), 1) % 64
    for b in range(4 * count):
        for part, src in enumerate((own, yr, yl)):
            acc_up = jnp.zeros((16, 128), F32)
            acc_down = jnp.zeros((16, 128), F32)
            for q in range(4):
                pair = src[4 * b + q]
                mask = (lane >= 16 * q) & (lane < 16 * q + 16)
                acc_up = jnp.where(mask, roll(pair, 16 * q - 48, 1), acc_up)
                acc_down = jnp.where(mask, roll(pair, 16 * q, 1), acc_down)
            up[b, 16 * part : 16 * part + 16] = acc_up
            down[b, 16 * part : 16 * part + 16] = acc_down


def clear(refs, low, high):
    for ref in refs:
        for p in (*range(low), *range(high, ref.shape[0])):
            ref[p] = jnp.zeros(ref.shape[1:], F32)


def outside1(iy, iz):
    row, lane = iota((48, 128), 0), iota((48, 128), 1)
    gone = ((row >= 16) & (row < 32) & (iy == 7)) | ((row >= 32) & (iy == 0))
    gone = gone | ((lane >= 64) & (lane < 80) & (iz == 7)) | ((lane >= 112) & (iz == 0))
    return gone | ((lane >= 80) & (lane < 112))


def spread1(ix, own, yl, yr, zl, zr, count, a, write):
    lane = iota((48, 128), 1)
    even = lane // 16 % 2 == 0
    for b in range(4):
        block = 8 * jnp.bitwise_xor(ix, b) + 4
        left, right = roll(zl[count * b + a], 48, 1), zr[count * b + a]
        sides = (jnp.where(even, right, left), jnp.where(even, left, right))
        for q in range(4):
            s = 4 * (count * b + a) + q
            pair = jnp.concatenate([own[s], yr[s], yl[s]], axis=0)
            for h in range(2):
                at = 16 * (q + 4 * h)
                side = roll(sides[q % 2], 64 - at, 1)
                value = jnp.where(lane < 64, roll(pair, 64 * h, 1), side)
                write(block + q + 4 * h, value)


def known2(shape):
    lane = iota(shape, 1)
    return (lane < 40) | (lane >= 120)


def to_second(tall, out, values, fill):
    def store(i, value):
        tall[pl.ds(pl.multiple_of(48 * i, 48), 48), :] = value

    planes(0, 16, lambda i: values(2 * i + 4) + values(2 * i + 5), store, 4)
    halves = tall[pl.ds(0, 384, stride=2), :] + tall[pl.ds(1, 384, stride=2), :]
    coarse = dot(halves, jnp.where(known2((128, 128)), pair_matrix(128), 0.0))
    for i in range(16):
        out[i + 4] = jnp.where(known2((24, 128)), coarse[24 * i : 24 * i + 24], fill)


def to_third(tall, small, write, values):
    for i in range(8):
        tall[24 * i : 24 * i + 24] = values(2 * i + 4) + values(2 * i + 5)
    halves = tall[pl.ds(0, 96, stride=2), :] + tall[pl.ds(1, 96, stride=2), :]
    spread = jnp.where(iota((128, 128), 0) // 2 == iota((128, 128), 1) % 16, 0.125, 0.0)
    small[0:96] = dot(halves, spread)
    group = iota((12, 128), 1) // 16
    packed = jnp.zeros((12, 128), F32)
    for i in range(8):
        packed = jnp.where(group == i, small[12 * i : 12 * i + 12], packed)
    small[0:12] = packed
    write(slice(0, 2), small[10:12])
    write(slice(2, 8), small[0:6])


def cut1(ix, src, out):
    for p in range(16):
        out[p, 0:20] = src[8 * ix + p, 0:20]
        out[p, 20:24] = src[8 * ix + p, 44:48]


def cut2(ix, src, out):
    for p in range(12):
        out[p, 0:12] = src[4 * ix + p, 0:12]
        out[p, 12:16] = src[4 * ix + p, 20:24]


def static_kernel(
    pos, own, yl, yr, zl, zr,
    coarsest, k1, w1, cy1, cz1, d1, k2, w2, cy2, cz2, d2,
    k1n, w1n, cy1n, cz1n, k2n, w2n, cy2n, cz2n,
    m1, m2, tall, small,
):
    ix, iy, iz = pos[0], pos[1], pos[2]
    gone = outside1(iy, iz)
    clear((k1, w1, cy1, cz1), 4, 36)
    clear((k2, w2, cy2, cz2), 4, 20)

    def write_m(p, value):
        m1[p] = jnp.where(gone, OUTSIDE, value)

    def write_k(p, value):
        k1[p] = jnp.where(gone, 0.0, 0.125 * value)

    spread1(ix, own, yl, yr, zl, zr, 2, 0, write_m)
    spread1(ix, own, yl, yr, zl, zr, 2, 1, write_k)
    coefficients(4, 36, 8, k1, None, m1, d1, w1, None, cy1, cz1)
    to_second(tall, m2, lambda p: m1[p], OUTSIDE)
    to_second(tall, k2, lambda p: 0.25 * k1[p], 0.0)
    coefficients(4, 20, 16, k2, None, m2, d2, w2, None, cy2, cz2)

    def write(slot):
        def put(where, value):
            coarsest[slot, where] = value

        return put

    to_third(tall, small, write(0), lambda p: m2[p])
    to_third(tall, small, write(1), lambda p: 0.25 * k2[p])
    for src, out in ((k1, k1n), (w1, w1n), (cy1, cy1n), (cz1, cz1n)):
        cut1(ix, src, out)
    for src, out in ((k2, k2n), (w2, w2n), (cy2, cy2n), (cz2, cz2n)):
        cut2(ix, src, out)


def middle_kernel(
    pos, own, yl, yr, zl, zr, coarsest, k1, w1, cy1, cz1, d1, k2, w2, cy2, cz2, d2,
    message, v1n, g1n, v2n, g2n,
    f1, g1, v1, f2, g2, v2, tall, small,
):
    ix, iy, iz = pos[0], pos[1], pos[2]
    gone = outside1(iy, iz)
    clear((g1, v1), 4, 36)
    clear((g2, v2), 4, 20)

    def write(p, value):
        value = jnp.where(gone, 0.0, value)
        f1[p] = value
        g1[p] = w1[p] * value

    spread1(ix, own, yl, yr, zl, zr, 1, 0, write)
    sweep(4, 36, 16, k1, w1, g1, cy1, cz1, g1, v1)

    def residual1(p):
        total, centre = neighbours(p, k1, cy1, cz1, v1)
        return jnp.where(gone, 0.0, f1[p] + total - d1[p] * centre)

    to_second(tall, f2, residual1, 0.0)
    for p in range(4, 20):
        g2[p] = w2[p] * f2[p]
    sweep(4, 20, 16, k2, w2, g2, cy2, cz2, g2, v2)
    row24 = iota((24, 128), 0)
    gone2 = ((row24 >= 8) & (row24 < 16) & (iy == 7)) | ((row24 >= 16) & (iy == 0))

    def residual2(p):
        total, centre = neighbours(p, k2, cy2, cz2, v2)
        return jnp.where(gone2, 0.0, f2[p] + total - d2[p] * centre)

    def put(where, value):
        message[0, where] = value

    to_third(tall, small, put, residual2)
    message[1] = coarsest[0]
    message[2] = coarsest[1]
    cut1(ix, v1, v1n)
    cut1(ix, g1, g1n)
    cut2(ix, v2, v2n)
    cut2(ix, g2, g2n)


def duplicate(out, base, rows, first, count):
    value = rows[first : first + count]
    out[pl.ds(base, count, stride=2), :] = value
    out[pl.ds(base + 1, count, stride=2), :] = value


def last_kernel(
    pos, own, first, second, v0, w0, g0, k0, cy0, cz0, v1, g1, v2, g2, k1, w1, cy1, cz1, k2, w2, cy2, cz2,
    out,
    k3, f3, m3, w3, g3, cy3, cz3, a3, rows, dup, a2, b2, a1, b1, wide, low, high, a0, b0,
):
    ix, iy, iz = pos[0], pos[1], pos[2]
    row = iota((24, 128), 0) + 4 * iy - 10
    lane = iota((24, 128), 1)
    gone = (row < 0) | (row >= 32) | ((lane >= 32) & (lane < 112))
    gone = gone | ((lane >= 16) & (lane < 32) & (iz == 7)) | ((lane >= 112) & (iz == 0))
    clear((k3, g3, a3), 2, 10)
    crossed = (iy // 2) % 2 == 0

    def stack(index):
        one, two = first[index], second[index]
        ahead, behind = jnp.where(crossed, two, one), jnp.where(crossed, one, two)
        ahead = jnp.where(iy == 1, roll(ahead, 4, 0), ahead)
        behind = jnp.where(iy == 6, roll(behind, 4, 0), behind)
        return jnp.concatenate([ahead, own[index], behind], axis=0)

    for a, (ref, fill) in enumerate(((f3, 0.0), (m3, OUTSIDE), (k3, 0.0))):
        here, left, right = (stack(3 * z + a) for z in range(3))
        for x in range(8):
            value = jnp.where(
                lane < 16,
                roll(here, -16 * x, 1),
                jnp.where(lane < 64, roll(right, 16 - 16 * x, 1), roll(left, 112 - 16 * x, 1)),
            )
            ref[x + 2] = jnp.where(gone, fill, value)
    coefficients(2, 10, 8, k3, f3, m3, None, w3, g3, cy3, cz3)
    field = [g3[p] for p in range(1, 11)]
    for _ in range(COARSE_SWEEPS - 1):
        inner = []
        for p in range(2, 10):
            behind, here, ahead = field[p - 2 : p + 1]
            total, _ = neighbours(p, k3, cy3, cz3, {p: here, p - 1: behind, p + 1: ahead})
            inner.append(KEEP * here + g3[p] + w3[p] * total)
        field = [field[0], *inner, field[9]]
    for p in range(8):
        a3[p + 2] = field[p + 1]

    src, column = iota((128, 128), 0), iota((128, 128), 1)
    to2 = jnp.where(
        ((column < 40) & (src == column // 2)) | ((column >= 120) & (src == 64 + column // 2)), 1.0, 0.0
    )
    for x in range(6):
        rows[24 * x : 24 * x + 24] = a3[2 * ix + x]
    rows[0:144] = dot(rows[0:144], to2)
    for x in range(6):
        duplicate(dup, 16 * x, rows, 24 * x + 10, 6)
        duplicate(dup, 16 * x + 12, rows, 24 * x + 8, 2)
        both = dup[16 * x : 16 * x + 16]
        a2[2 * x] = v2[2 * x] + both
        a2[2 * x + 1] = v2[2 * x + 1] + both
    sweep(1, 11, 10, k2, w2, g2, cy2, cz2, a2, b2)
    sweep(2, 10, 8, k2, w2, g2, cy2, cz2, b2, a2)

    to1 = jnp.where(
        ((column < 80) & (src == column // 2)) | ((column >= 112) & (src == 64 + column // 2)), 1.0, 0.0
    )
    for x in range(8):
        rows[16 * x : 16 * x + 16] = a2[x + 2]
    rows[0:128] = dot(rows[0:128], to1)
    for x in range(8):
        duplicate(dup, 24 * x, rows, 16 * x, 10)
        duplicate(dup, 24 * x + 20, rows, 16 * x + 14, 2)
        both = dup[24 * x : 24 * x + 24]
        a1[2 * x] = v1[2 * x] + both
        a1[2 * x + 1] = v1[2 * x + 1] + both
    sweep(2, 14, 12, k1, w1, g1, cy1, cz1, a1, b1)
    sweep(3, 13, 10, k1, w1, g1, cy1, cz1, b1, a1)

    to0 = jnp.where(iota((128, 256), 0) == iota((128, 256), 1) // 2, 1.0, 0.0)
    for x in range(10):
        rows[24 * x : 24 * x + 24] = a1[x + 3]
    wide[...] = dot(rows[0:240], to0)
    for x in range(10):
        for half, lanes in ((low, slice(0, 128)), (high, slice(128, 256))):
            mid = wide[24 * x : 24 * x + 18, lanes]
            half[pl.ds(0, 18, stride=2), :] = mid
            half[pl.ds(1, 18, stride=2), :] = mid
            ahead = wide[24 * x + 22 : 24 * x + 24, lanes]
            half[pl.ds(36, 2, stride=2), :] = ahead
            half[pl.ds(37, 2, stride=2), :] = ahead
            for p in (2 * x + 2, 2 * x + 3):
                a0[p, :, lanes] = v0[p, :, lanes] + half[...]
    sweep(3, 21, 9, k0, w0, g0, cy0, cz0, a0, b0)

    def values(p):
        total, centre = neighbours(p, k0, cy0, cz0, b0)
        return (KEEP * centre + g0[p] + w0[p] * total)[0:32, 0:128]

    def store(p, value):
        out[p - 4] = value

    planes(4, 20, values, store, 8)


VMEM = pl.BlockSpec(memory_space=pltpu.VMEM)
SMEM = pl.BlockSpec(memory_space=pltpu.SMEM)


COARSE_TARGETS = ((2, 3, 0, 1, 6, 7, 4, 5), (1, 0, 4, 5, 2, 3, 7, 6))


def call(kernel, outs, scratch, *args, pos=None):
    specs = [VMEM] * len(args)
    if pos is not None:
        args = (pos,) + args
        specs = [SMEM] + specs
    return pl.pallas_call(
        kernel,
        out_shape=[jax.ShapeDtypeStruct(s, F32) for s in outs],
        in_specs=specs,
        out_specs=[VMEM] * len(outs),
        scratch_shapes=[pltpu.VMEM(s, F32) for s in scratch],
        compiler_params=pltpu.CompilerParams(vmem_limit_bytes=16 * 1024 * 1024),
        name=getattr(kernel, "__name__", "pack_z1_kernel"),
    )(*args)


def swap(x, axis, bits):
    size = lax.axis_size(axis)
    return lax.ppermute(x, axis, [(i, i ^ bits) for i in range(size)])


FULL, SIDES = (24, 40, 256), (3, 40, 128)
ONE, TWO, THREE = (40, 48, 128), (24, 24, 128), (12, 24, 128)
NEAR1, NEAR2 = (16, 24, 128), (12, 16, 128)
TALL = (768, 128)


def gather_x(x):
    return jnp.concatenate([x] + [swap(x, "gx", bits) for bits in (1, 2, 3)])


def both_sides(up, down, axis):
    size = lax.axis_size(axis)
    even = lax.axis_index(axis) % 2 == 0
    far = [(i, (i + 1) % size if i % 2 else (i - 1) % size) for i in range(size)]
    there = lax.ppermute(jnp.where(even, down, up), axis, far)
    here = swap(jnp.where(even, up, down), axis, 1)
    return jnp.where(even, there, here), jnp.where(even, here, there)


def pack_z1(count, own, yl, yr):
    kernel = functools.partial(pack_z1_kernel, count)
    return call(kernel, [(4 * count, 48, 128)] * 2, [], own, yl, yr)


def ordered(x, *others):
    return lax.optimization_barrier((x, *others))[0]


def per_device(f, k, m):
    pos = jnp.stack([lax.axis_index("gx"), lax.axis_index("gy"), lax.axis_index("gz")])
    pos = pos.astype(jnp.int32)

    up = jnp.concatenate([f[13:], m[13:], k[12:]])
    down = jnp.concatenate([f[:3], m[:3], k[:4]])
    xl, xr = both_sides(up, down, "gx")
    (brick,) = call(
        coarse_kernel, [(8, 16, 128)], [(256, 128)], k, m
    )
    static = gather_x(brick)

    yl, yr = both_sides(*call(pack_y_kernel, [(ROW_COUNT, 128)] * 2, [], f, k, m, xl, xr), "gy")
    fa, ka, ma, up, down = call(
        pack_z_kernel, [(24, 40, 128)] * 3 + [SIDES] * 2, [], f, k, m, xl, xr, yl, yr
    )
    zl, zr = both_sides(up, down, "gz")
    static_yl, static_yr = both_sides(static, static, "gy")
    brick, *level0 = call(
        fine_kernel,
        [(4, 16, 128)] + [FULL] * 6,
        [FULL] * 3 + [(256, 128)],
        fa, ka, ma, zl, zr,
        pos=pos,
    )
    static_up, static_down = pack_z1(2, static, static_yl, static_yr)

    own = gather_x(brick)
    static_zl, static_zr = both_sides(static_up, static_down, "gz")
    coarsest, *static = call(
        static_kernel,
        [(2, 8, 128)] + [ONE] * 5 + [TWO] * 5 + [NEAR1] * 4 + [NEAR2] * 4,
        [ONE, TWO, TALL, (96, 128)],
        static, static_yl, static_yr, static_zl, static_zr,
        pos=pos,
    )
    whole, near = static[:10], static[10:]
    yl, yr = both_sides(own, own, "gy")
    up, down = pack_z1(1, own, yl, yr)
    zl, zr = both_sides(up, down, "gz")
    message, *vary = call(
        middle_kernel,
        [(3, 8, 128)] + [NEAR1] * 2 + [NEAR2] * 2,
        [ONE] * 3 + [TWO] * 3 + [TALL, (96, 128)],
        own, yl, yr, zl, zr, coarsest, *whole,
        pos=pos,
    )

    own = jnp.concatenate([message, *both_sides(message, message, "gz")])
    first, second = (lax.ppermute(own, "gy", list(enumerate(t))) for t in COARSE_TARGETS)
    return call(
        last_kernel,
        [(16, 32, 128)],
        [THREE] * 8 + [(240, 128), (192, 128)] + [NEAR2] * 2 + [NEAR1] * 2
        + [(240, 256), (40, 128), (40, 128)] + [FULL] * 2,
        own, first, second, *level0, *vary, *near,
        pos=pos,
    )[0]


def solution(mesh):
    placed = (P("gx", "gy", "gz"), P("gx", "gy", "gz"), P("gx", "gy", "gz"))
    return jax.shard_map(
        per_device, mesh=mesh, in_specs=placed, out_specs=P("gx", "gy", "gz"), check_vma=False
    )
```

```python
import functools

import jax
import jax.numpy as jnp
from jax import lax
from jax.experimental import pallas as pl
from jax.experimental.pallas import tpu as pltpu
from jax.sharding import PartitionSpec as P

SWEEPS = 2
COARSE_SWEEPS = 8
OMEGA = 2.0 / 3.0
KEEP = 1.0 - OMEGA
OUTSIDE = 1e30
LIMIT = 1e29
F32 = jnp.float32
BF16 = jnp.bfloat16


def dot(a, b):
    high = a.astype(BF16)
    rest = a - high.astype(F32)
    middle = rest.astype(BF16)
    low = (rest - middle.astype(F32)).astype(BF16)
    terms = jnp.concatenate([high, middle, low], axis=1)
    matrix = b.astype(BF16)
    return jnp.dot(terms, jnp.concatenate([matrix] * 3, axis=0), preferred_element_type=F32)


def iota(shape, dim):
    return lax.broadcasted_iota(jnp.int32, shape, dim)


def roll(x, shift, axis):
    size = x.shape[axis]
    shift = shift % size
    return x if shift == 0 else pltpu.roll(x, shift, axis)


def after(x, axis):
    return roll(x, -1, axis)


def before(x, axis):
    return roll(x, 1, axis)


def planes(low, high, values, store, group):
    def run(first, count):
        found = [values(first + i) for i in range(count)]
        for i, value in enumerate(found):
            store(first + i, value)

    whole = (high - low) // group
    if whole == 1:
        run(low, group)
    elif whole:

        def step(index, carry):
            run(low + index * group, group)
            return carry

        lax.fori_loop(0, whole, step, 0)
    if (high - low) % group:
        run(low + whole * group, (high - low) % group)


def coefficients(low, high, group, k, f, m, d, w, g, cy, cz):
    def values(p):
        here = k[p]
        y = here + after(here, 0)
        z = here + after(here, 1)
        diagonal = m[p] + (k[p - 1] + here) + (here + k[p + 1])
        diagonal = diagonal + y + before(y, 0) + z + before(z, 1)
        weight = jnp.where(m[p] < LIMIT, OMEGA / diagonal, 0.0)
        return y, z, weight, diagonal, None if f is None else weight * f[p]

    def store(p, found):
        cy[p], cz[p], w[p] = found[:3]
        if d is not None:
            d[p] = found[3]
        if f is not None:
            g[p] = found[4]

    planes(low, high, values, store, group)


def neighbours(p, k, cy, cz, v):
    here, centre, y, z = k[p], v[p], cy[p], cz[p]
    total = (k[p - 1] + here) * v[p - 1] + (here + k[p + 1]) * v[p + 1]
    total = total + y * after(centre, 0) + before(y * centre, 0)
    total = total + z * after(centre, 1) + before(z * centre, 1)
    return total, centre


def own_neighbours(p, k, cy, cz, v):
    rows, lanes = slice(0, 32), slice(0, 128)
    here = k[p, rows, lanes]
    total = (k[p - 1, rows, lanes] + here) * v[p - 1, rows, lanes]
    total = total + (here + k[p + 1, rows, lanes]) * v[p + 1, rows, lanes]
    centre, y = v[p, :, lanes], cy[p, :, lanes]
    total = total + (y * after(centre, 0) + before(y * centre, 0))[rows]
    across, z = v[p, rows], cz[p, rows]
    total = total + (z * after(across, 1) + before(z * across, 1))[:, lanes]
    return total, centre[rows]


def sweep(low, high, group, k, w, g, cy, cz, v, out):
    def values(p):
        total, centre = neighbours(p, k, cy, cz, v)
        return KEEP * centre + g[p] + w[p] * total

    def store(p, value):
        out[p] = value

    planes(low, high, values, store, group)


def reach(p):
    away = max(0, 4 - p, p - 19)
    return max(0, 3 - away), 4 - away


def row_table():
    table, base = [], 0
    for p in range(24):
        three, four = reach(p)
        table.append((base, base + three, base + 2 * three))
        base += 2 * three + four
    return table, base


ROWS, ROW_COUNT = row_table()


def pack_y_kernel(f, k, m, xl, xr, up, down):
    for p in range(24):
        if p < 4:
            refs = ((xl, p - 1), (xl, 2 + p), (xl, 6 + p))
        elif p < 20:
            refs = ((f, p - 4), (m, p - 4), (k, p - 4))
        else:
            refs = ((xr, p - 20), (xr, p - 17), (xr, p - 14))
        for a, (ref, plane) in enumerate(refs):
            count, base = reach(p)[a // 2], ROWS[p][a]
            if count:
                up[base : base + count] = ref[plane, 32 - count : 32]
                down[base : base + count] = ref[plane, 0:count]


def pack_z_kernel(f, k, m, xl, xr, yl, yr, fa, ka, ma, up, down):
    lane = iota((40, 128), 1)
    zero = jnp.zeros((32, 128), F32)
    faces = [[None, None] for _ in range(3)]
    for p in range(24):
        g, i = p // 16, p % 16
        if p < 4:
            own = (xl[p - 1] if p else zero, xl[2 + p] if p else zero, xl[6 + p])
        elif p < 20:
            own = (f[p - 4], m[p - 4], k[p - 4])
        else:
            own = (xr[p - 20] if p < 23 else zero, xr[p - 17] if p < 23 else zero, xr[p - 14])
        for a, out in enumerate((fa, ma, ka)):
            count, base = reach(p)[a // 2], ROWS[p][a]
            out[p, 0:32] = own[a]
            out[p, 32:40] = jnp.zeros((8, 128), F32)
            if count:
                out[p, 32 : 32 + count] = yr[base : base + count]
                out[p, 40 - count : 40] = yl[base : base + count]
            moved = roll(out[p], 8 * i + 4, 1)
            faces[a][g] = moved if i == 0 else jnp.where(lane // 8 == i, moved, faces[a][g])
    front = lane % 8 < 4
    source, screening, conductivity = faces
    pairs = ((source[0], screening[0]), (source[1], screening[1]), conductivity)
    for g, (one, two) in enumerate(pairs):
        up[g] = jnp.where(front, one, roll(two, 4, 1))
        down[g] = jnp.where(front, roll(one, -4, 1), two)


def pair_matrix(columns):
    return jnp.where(iota((128, columns), 0) // 2 == iota((128, columns), 1) % 64, 0.125, 0.0)


def coarse_kernel(k, m, message, tall):
    pairs = pair_matrix(128)
    for slot, ref in enumerate((m, k)):
        for i in range(8):
            tall[32 * i : 32 * i + 32] = ref[2 * i] + ref[2 * i + 1]
        halve_and_pack(tall, pairs, message, 4 * slot)


def halve_and_pack(tall, pairs, message, first):
    lane16 = iota((16, 128), 1)
    halves = tall[pl.ds(0, 128, stride=2), :] + tall[pl.ds(1, 128, stride=2), :]
    coarse = dot(halves, pairs)
    for i in range(4):
        message[first + i] = jnp.where(
            lane16 < 64, coarse[16 * i : 16 * i + 16], coarse[16 * i + 64 : 16 * i + 80]
        )


def fine_kernel(pos, fa, ka, ma, zl, zr, message, v_out, w, g, k, cy, cz, f, m, d, tall):
    ix, iy, iz = pos[0], pos[1], pos[2]
    row = iota((40, 128), 0)
    lane = iota((40, 128), 1)
    far = ((row >= 32) & (row < 36) & (iy == 7)) | ((row >= 36) & (iy == 0))
    beside = ((lane < 4) & (iz < 7)) | ((lane >= 124) & (iz > 0))
    inner = (lane < 3) | (lane > 124)
    front = lane % 8 < 4
    ones = [jnp.where(front, zl[g], roll(zr[g], 4, 1)) for g in range(3)]
    twos = [jnp.where(front, roll(zl[g], -4, 1), zr[g]) for g in range(3)]
    faces = (ones[:2], twos[:2], (ones[2], twos[2]))
    for p in range(24):
        group, i = p // 16, p % 16
        absent = False
        if p < 4:
            absent = ix == 0
        elif p >= 20:
            absent = ix == 3
        gone = far | absent
        three = reach(p)[0]
        unknown = (row >= 32 + three) & (row < 40 - three)
        for a, (src, out) in enumerate(((fa, f), (ma, m), (ka, k))):
            if a == 1 and p in (0, 23):
                out[p] = jnp.full((40, 256), OUTSIDE, F32)
                continue
            side = roll(faces[a][group], -8 * i - 4, 1)
            own = src[p]
            fill = OUTSIDE if a == 1 else 0.0
            if a == 2:
                here, there = gone, gone | ~beside
                own, side = 0.5 * own, 0.5 * side
            else:
                here = gone | unknown
                there = here | ~(beside & inner)
            out[p, :, 0:128] = jnp.where(here, fill, own)
            out[p, :, 128:256] = jnp.where(there, fill, side)
    coefficients(1, 23, 11, k, f, m, d, w, g, cy, cz)
    sweep(2, 22, 10, k, w, g, cy, cz, g, v_out)

    def residual(p):
        total, centre = own_neighbours(p, k, cy, cz, v_out)
        return f[p, 0:32, 0:128] + total - d[p, 0:32, 0:128] * centre

    def values(i):
        return residual(2 * i + 4) + residual(2 * i + 5)

    def store(i, value):
        tall[pl.ds(pl.multiple_of(32 * i, 32), 32), :] = value

    planes(0, 8, values, store, 8)
    halve_and_pack(tall, pair_matrix(128), message, 0)


def pack_z1_kernel(count, own, yl, yr, up, down):
    lane = iota((16, 128), 1) % 64
    for b in range(4 * count):
        for part, src in enumerate((own, yr, yl)):
            acc_up = jnp.zeros((16, 128), F32)
            acc_down = jnp.zeros((16, 128), F32)
            for q in range(4):
                pair = src[4 * b + q]
                mask = (lane >= 16 * q) & (lane < 16 * q + 16)
                acc_up = jnp.where(mask, roll(pair, 16 * q - 48, 1), acc_up)
                acc_down = jnp.where(mask, roll(pair, 16 * q, 1), acc_down)
            up[b, 16 * part : 16 * part + 16] = acc_up
            down[b, 16 * part : 16 * part + 16] = acc_down


def clear(refs, low, high):
    for ref in refs:
        for p in (*range(low), *range(high, ref.shape[0])):
            ref[p] = jnp.zeros(ref.shape[1:], F32)


def outside1(iy, iz):
    row, lane = iota((48, 128), 0), iota((48, 128), 1)
    gone = ((row >= 16) & (row < 32) & (iy == 7)) | ((row >= 32) & (iy == 0))
    gone = gone | ((lane >= 64) & (lane < 80) & (iz == 7)) | ((lane >= 112) & (iz == 0))
    return gone | ((lane >= 80) & (lane < 112))


def spread1(ix, own, yl, yr, zl, zr, count, a, write):
    lane = iota((48, 128), 1)
    even = lane // 16 % 2 == 0
    for b in range(4):
        block = 8 * jnp.bitwise_xor(ix, b) + 4
        left, right = roll(zl[count * b + a], 48, 1), zr[count * b + a]
        sides = (jnp.where(even, right, left), jnp.where(even, left, right))
        for q in range(4):
            s = 4 * (count * b + a) + q
            pair = jnp.concatenate([own[s], yr[s], yl[s]], axis=0)
            for h in range(2):
                at = 16 * (q + 4 * h)
                side = roll(sides[q % 2], 64 - at, 1)
                value = jnp.where(lane < 64, roll(pair, 64 * h, 1), side)
                write(block + q + 4 * h, value)


def known2(shape):
    lane = iota(shape, 1)
    return (lane < 40) | (lane >= 120)


def to_second(tall, out, values, fill):
    def store(i, value):
        tall[pl.ds(pl.multiple_of(48 * i, 48), 48), :] = value

    planes(0, 16, lambda i: values(2 * i + 4) + values(2 * i + 5), store, 4)
    halves = tall[pl.ds(0, 384, stride=2), :] + tall[pl.ds(1, 384, stride=2), :]
    coarse = dot(halves, jnp.where(known2((128, 128)), pair_matrix(128), 0.0))
    for i in range(16):
        out[i + 4] = jnp.where(known2((24, 128)), coarse[24 * i : 24 * i + 24], fill)


def to_third(tall, small, write, values):
    for i in range(8):
        tall[24 * i : 24 * i + 24] = values(2 * i + 4) + values(2 * i + 5)
    halves = tall[pl.ds(0, 96, stride=2), :] + tall[pl.ds(1, 96, stride=2), :]
    spread = jnp.where(iota((128, 128), 0) // 2 == iota((128, 128), 1) % 16, 0.125, 0.0)
    small[0:96] = dot(halves, spread)
    group = iota((12, 128), 1) // 16
    packed = jnp.zeros((12, 128), F32)
    for i in range(8):
        packed = jnp.where(group == i, small[12 * i : 12 * i + 12], packed)
    small[0:12] = packed
    write(slice(0, 2), small[10:12])
    write(slice(2, 8), small[0:6])


def cut1(ix, src, out):
    for p in range(16):
        out[p, 0:20] = src[8 * ix + p, 0:20]
        out[p, 20:24] = src[8 * ix + p, 44:48]


def cut2(ix, src, out):
    for p in range(12):
        out[p, 0:12] = src[4 * ix + p, 0:12]
        out[p, 12:16] = src[4 * ix + p, 20:24]


def static_kernel(
    pos, own, yl, yr, zl, zr,
    coarsest, k1, w1, cy1, cz1, d1, k2, w2, cy2, cz2, d2,
    k1n, w1n, cy1n, cz1n, k2n, w2n, cy2n, cz2n,
    m1, m2, tall, small,
):
    ix, iy, iz = pos[0], pos[1], pos[2]
    gone = outside1(iy, iz)
    clear((k1, w1, cy1, cz1), 4, 36)
    clear((k2, w2, cy2, cz2), 4, 20)

    def write_m(p, value):
        m1[p] = jnp.where(gone, OUTSIDE, value)

    def write_k(p, value):
        k1[p] = jnp.where(gone, 0.0, 0.125 * value)

    spread1(ix, own, yl, yr, zl, zr, 2, 0, write_m)
    spread1(ix, own, yl, yr, zl, zr, 2, 1, write_k)
    coefficients(4, 36, 8, k1, None, m1, d1, w1, None, cy1, cz1)
    to_second(tall, m2, lambda p: m1[p], OUTSIDE)
    to_second(tall, k2, lambda p: 0.25 * k1[p], 0.0)
    coefficients(4, 20, 16, k2, None, m2, d2, w2, None, cy2, cz2)

    def write(slot):
        def put(where, value):
            coarsest[slot, where] = value

        return put

    to_third(tall, small, write(0), lambda p: m2[p])
    to_third(tall, small, write(1), lambda p: 0.25 * k2[p])
    for src, out in ((k1, k1n), (w1, w1n), (cy1, cy1n), (cz1, cz1n)):
        cut1(ix, src, out)
    for src, out in ((k2, k2n), (w2, w2n), (cy2, cy2n), (cz2, cz2n)):
        cut2(ix, src, out)


def middle_kernel(
    pos, own, yl, yr, zl, zr, coarsest, k1, w1, cy1, cz1, d1, k2, w2, cy2, cz2, d2,
    message, v1n, g1n, v2n, g2n,
    f1, g1, v1, f2, g2, v2, tall, small,
):
    ix, iy, iz = pos[0], pos[1], pos[2]
    gone = outside1(iy, iz)
    clear((g1, v1), 4, 36)
    clear((g2, v2), 4, 20)

    def write(p, value):
        value = jnp.where(gone, 0.0, value)
        f1[p] = value
        g1[p] = w1[p] * value

    spread1(ix, own, yl, yr, zl, zr, 1, 0, write)
    sweep(4, 36, 16, k1, w1, g1, cy1, cz1, g1, v1)

    def residual1(p):
        total, centre = neighbours(p, k1, cy1, cz1, v1)
        return jnp.where(gone, 0.0, f1[p] + total - d1[p] * centre)

    to_second(tall, f2, residual1, 0.0)
    for p in range(4, 20):
        g2[p] = w2[p] * f2[p]
    sweep(4, 20, 16, k2, w2, g2, cy2, cz2, g2, v2)
    row24 = iota((24, 128), 0)
    gone2 = ((row24 >= 8) & (row24 < 16) & (iy == 7)) | ((row24 >= 16) & (iy == 0))

    def residual2(p):
        total, centre = neighbours(p, k2, cy2, cz2, v2)
        return jnp.where(gone2, 0.0, f2[p] + total - d2[p] * centre)

    def put(where, value):
        message[0, where] = value

    to_third(tall, small, put, residual2)
    message[1] = coarsest[0]
    message[2] = coarsest[1]
    cut1(ix, v1, v1n)
    cut1(ix, g1, g1n)
    cut2(ix, v2, v2n)
    cut2(ix, g2, g2n)


def duplicate(out, base, rows, first, count):
    value = rows[first : first + count]
    out[pl.ds(base, count, stride=2), :] = value
    out[pl.ds(base + 1, count, stride=2), :] = value


def last_kernel(
    pos, own, first, second, v0, w0, g0, k0, cy0, cz0, v1, g1, v2, g2, k1, w1, cy1, cz1, k2, w2, cy2, cz2,
    out,
    k3, f3, m3, w3, g3, cy3, cz3, a3, rows, dup, a2, b2, a1, b1, wide, low, high, a0, b0,
):
    ix, iy, iz = pos[0], pos[1], pos[2]
    row = iota((24, 128), 0) + 4 * iy - 10
    lane = iota((24, 128), 1)
    gone = (row < 0) | (row >= 32) | ((lane >= 32) & (lane < 112))
    gone = gone | ((lane >= 16) & (lane < 32) & (iz == 7)) | ((lane >= 112) & (iz == 0))
    clear((k3, g3, a3), 2, 10)
    crossed = (iy // 2) % 2 == 0

    def stack(index):
        one, two = first[index], second[index]
        ahead, behind = jnp.where(crossed, two, one), jnp.where(crossed, one, two)
        ahead = jnp.where(iy == 1, roll(ahead, 4, 0), ahead)
        behind = jnp.where(iy == 6, roll(behind, 4, 0), behind)
        return jnp.concatenate([ahead, own[index], behind], axis=0)

    for a, (ref, fill) in enumerate(((f3, 0.0), (m3, OUTSIDE), (k3, 0.0))):
        here, left, right = (stack(3 * z + a) for z in range(3))
        for x in range(8):
            value = jnp.where(
                lane < 16,
                roll(here, -16 * x, 1),
                jnp.where(lane < 64, roll(right, 16 - 16 * x, 1), roll(left, 112 - 16 * x, 1)),
            )
            ref[x + 2] = jnp.where(gone, fill, value)
    coefficients(2, 10, 8, k3, f3, m3, None, w3, g3, cy3, cz3)
    field = [g3[p] for p in range(1, 11)]
    for _ in range(COARSE_SWEEPS - 1):
        inner = []
        for p in range(2, 10):
            behind, here, ahead = field[p - 2 : p + 1]
            total, _ = neighbours(p, k3, cy3, cz3, {p: here, p - 1: behind, p + 1: ahead})
            inner.append(KEEP * here + g3[p] + w3[p] * total)
        field = [field[0], *inner, field[9]]
    for p in range(8):
        a3[p + 2] = field[p + 1]

    src, column = iota((128, 128), 0), iota((128, 128), 1)
    to2 = jnp.where(
        ((column < 40) & (src == column // 2)) | ((column >= 120) & (src == 64 + column // 2)), 1.0, 0.0
    )
    for x in range(6):
        rows[24 * x : 24 * x + 24] = a3[2 * ix + x]
    rows[0:144] = dot(rows[0:144], to2)
    for x in range(6):
        duplicate(dup, 16 * x, rows, 24 * x + 10, 6)
        duplicate(dup, 16 * x + 12, rows, 24 * x + 8, 2)
        both = dup[16 * x : 16 * x + 16]
        a2[2 * x] = v2[2 * x] + both
        a2[2 * x + 1] = v2[2 * x + 1] + both
    sweep(1, 11, 10, k2, w2, g2, cy2, cz2, a2, b2)
    sweep(2, 10, 8, k2, w2, g2, cy2, cz2, b2, a2)

    to1 = jnp.where(
        ((column < 80) & (src == column // 2)) | ((column >= 112) & (src == 64 + column // 2)), 1.0, 0.0
    )
    for x in range(8):
        rows[16 * x : 16 * x + 16] = a2[x + 2]
    rows[0:128] = dot(rows[0:128], to1)
    for x in range(8):
        duplicate(dup, 24 * x, rows, 16 * x, 10)
        duplicate(dup, 24 * x + 20, rows, 16 * x + 14, 2)
        both = dup[24 * x : 24 * x + 24]
        a1[2 * x] = v1[2 * x] + both
        a1[2 * x + 1] = v1[2 * x + 1] + both
    sweep(2, 14, 12, k1, w1, g1, cy1, cz1, a1, b1)
    sweep(3, 13, 10, k1, w1, g1, cy1, cz1, b1, a1)

    to0 = jnp.where(iota((128, 256), 0) == iota((128, 256), 1) // 2, 1.0, 0.0)
    for x in range(10):
        rows[24 * x : 24 * x + 24] = a1[x + 3]
    wide[...] = dot(rows[0:240], to0)
    for x in range(10):
        for half, lanes in ((low, slice(0, 128)), (high, slice(128, 256))):
            mid = wide[24 * x : 24 * x + 18, lanes]
            half[pl.ds(0, 18, stride=2), :] = mid
            half[pl.ds(1, 18, stride=2), :] = mid
            ahead = wide[24 * x + 22 : 24 * x + 24, lanes]
            half[pl.ds(36, 2, stride=2), :] = ahead
            half[pl.ds(37, 2, stride=2), :] = ahead
            for p in (2 * x + 2, 2 * x + 3):
                a0[p, :, lanes] = v0[p, :, lanes] + half[...]
    sweep(3, 21, 9, k0, w0, g0, cy0, cz0, a0, b0)

    def values(p):
        total, centre = own_neighbours(p, k0, cy0, cz0, b0)
        return KEEP * centre + g0[p, 0:32, 0:128] + w0[p, 0:32, 0:128] * total

    def store(p, value):
        out[p - 4] = value

    planes(4, 20, values, store, 16)


VMEM = pl.BlockSpec(memory_space=pltpu.VMEM)
SMEM = pl.BlockSpec(memory_space=pltpu.SMEM)


COARSE_TARGETS = ((2, 3, 0, 1, 6, 7, 4, 5), (1, 0, 4, 5, 2, 3, 7, 6))


def call(kernel, outs, scratch, *args, pos=None):
    specs = [VMEM] * len(args)
    if pos is not None:
        args = (pos,) + args
        specs = [SMEM] + specs
    return pl.pallas_call(
        kernel,
        out_shape=[jax.ShapeDtypeStruct(s, F32) for s in outs],
        in_specs=specs,
        out_specs=[VMEM] * len(outs),
        scratch_shapes=[pltpu.VMEM(s, F32) for s in scratch],
        compiler_params=pltpu.CompilerParams(vmem_limit_bytes=16 * 1024 * 1024),
        name=getattr(kernel, "__name__", "pack_z1_kernel"),
    )(*args)


def swap(x, axis, bits):
    size = lax.axis_size(axis)
    return lax.ppermute(x, axis, [(i, i ^ bits) for i in range(size)])


FULL, SIDES = (24, 40, 256), (3, 40, 128)
ONE, TWO, THREE = (40, 48, 128), (24, 24, 128), (12, 24, 128)
NEAR1, NEAR2 = (16, 24, 128), (12, 16, 128)
TALL = (768, 128)


def gather_x(x):
    return jnp.concatenate([x] + [swap(x, "gx", bits) for bits in (1, 2, 3)])


def both_sides(up, down, axis):
    size = lax.axis_size(axis)
    even = lax.axis_index(axis) % 2 == 0
    far = [(i, (i + 1) % size if i % 2 else (i - 1) % size) for i in range(size)]
    there = lax.ppermute(jnp.where(even, down, up), axis, far)
    here = swap(jnp.where(even, up, down), axis, 1)
    return jnp.where(even, there, here), jnp.where(even, here, there)


def pack_z1(count, own, yl, yr):
    kernel = functools.partial(pack_z1_kernel, count)
    return call(kernel, [(4 * count, 48, 128)] * 2, [], own, yl, yr)


def ordered(x, *others):
    return lax.optimization_barrier((x, *others))[0]


def per_device(f, k, m):
    pos = jnp.stack([lax.axis_index("gx"), lax.axis_index("gy"), lax.axis_index("gz")])
    pos = pos.astype(jnp.int32)

    up = jnp.concatenate([f[13:], m[13:], k[12:]])
    down = jnp.concatenate([f[:3], m[:3], k[:4]])
    xl, xr = both_sides(up, down, "gx")
    (brick,) = call(
        coarse_kernel, [(8, 16, 128)], [(256, 128)], k, m
    )
    static = gather_x(brick)

    yl, yr = both_sides(*call(pack_y_kernel, [(ROW_COUNT, 128)] * 2, [], f, k, m, xl, xr), "gy")
    fa, ka, ma, up, down = call(
        pack_z_kernel, [(24, 40, 128)] * 3 + [SIDES] * 2, [], f, k, m, xl, xr, yl, yr
    )
    zl, zr = both_sides(up, down, "gz")
    static_yl, static_yr = both_sides(static, static, "gy")
    brick, *level0 = call(
        fine_kernel,
        [(4, 16, 128)] + [FULL] * 6,
        [FULL] * 3 + [(256, 128)],
        fa, ka, ma, zl, zr,
        pos=pos,
    )
    static_up, static_down = pack_z1(2, static, static_yl, static_yr)

    own = gather_x(brick)
    static_zl, static_zr = both_sides(static_up, static_down, "gz")
    coarsest, *static = call(
        static_kernel,
        [(2, 8, 128)] + [ONE] * 5 + [TWO] * 5 + [NEAR1] * 4 + [NEAR2] * 4,
        [ONE, TWO, TALL, (96, 128)],
        static, static_yl, static_yr, static_zl, static_zr,
        pos=pos,
    )
    whole, near = static[:10], static[10:]
    yl, yr = both_sides(own, own, "gy")
    up, down = pack_z1(1, own, yl, yr)
    zl, zr = both_sides(up, down, "gz")
    message, *vary = call(
        middle_kernel,
        [(3, 8, 128)] + [NEAR1] * 2 + [NEAR2] * 2,
        [ONE] * 3 + [TWO] * 3 + [TALL, (96, 128)],
        own, yl, yr, zl, zr, coarsest, *whole,
        pos=pos,
    )

    own = jnp.concatenate([message, *both_sides(message, message, "gz")])
    first, second = (lax.ppermute(own, "gy", list(enumerate(t))) for t in COARSE_TARGETS)
    return call(
        last_kernel,
        [(16, 32, 128)],
        [THREE] * 8 + [(240, 128), (192, 128)] + [NEAR2] * 2 + [NEAR1] * 2
        + [(240, 256), (40, 128), (40, 128)] + [FULL] * 2,
        own, first, second, *level0, *vary, *near,
        pos=pos,
    )[0]


def solution(mesh):
    placed = (P("gx", "gy", "gz"), P("gx", "gy", "gz"), P("gx", "gy", "gz"))
    return jax.shard_map(
        per_device, mesh=mesh, in_specs=placed, out_specs=P("gx", "gy", "gz"), check_vma=False
    )
```

```python
import functools

import jax
import jax.numpy as jnp
from jax import lax
from jax.experimental import pallas as pl
from jax.experimental.pallas import tpu as pltpu
from jax.sharding import PartitionSpec as P

SWEEPS = 2
COARSE_SWEEPS = 8
OMEGA = 2.0 / 3.0
KEEP = 1.0 - OMEGA
OUTSIDE = 1e30
LIMIT = 1e29
F32 = jnp.float32
BF16 = jnp.bfloat16


def dot(a, b):
    high = a.astype(BF16)
    rest = a - high.astype(F32)
    middle = rest.astype(BF16)
    low = (rest - middle.astype(F32)).astype(BF16)
    terms = jnp.concatenate([high, middle, low], axis=1)
    matrix = b.astype(BF16)
    return jnp.dot(terms, jnp.concatenate([matrix] * 3, axis=0), preferred_element_type=F32)


def iota(shape, dim):
    return lax.broadcasted_iota(jnp.int32, shape, dim)


def roll(x, shift, axis):
    size = x.shape[axis]
    shift = shift % size
    return x if shift == 0 else pltpu.roll(x, shift, axis)


def after(x, axis):
    return roll(x, -1, axis)


def before(x, axis):
    return roll(x, 1, axis)


def planes(low, high, values, store, group):
    def run(first, count):
        found = [values(first + i) for i in range(count)]
        for i, value in enumerate(found):
            store(first + i, value)

    whole = (high - low) // group
    if whole == 1:
        run(low, group)
    elif whole:

        def step(index, carry):
            run(low + index * group, group)
            return carry

        lax.fori_loop(0, whole, step, 0)
    if (high - low) % group:
        run(low + whole * group, (high - low) % group)


def coefficients(low, high, group, k, f, m, d, w, g, cy, cz):
    def values(p):
        here = k[p]
        y = here + after(here, 0)
        z = here + after(here, 1)
        diagonal = m[p] + (k[p - 1] + here) + (here + k[p + 1])
        diagonal = diagonal + y + before(y, 0) + z + before(z, 1)
        weight = jnp.where(m[p] < LIMIT, OMEGA / diagonal, 0.0)
        return y, z, weight, diagonal, None if f is None else weight * f[p]

    def store(p, found):
        cy[p], cz[p], w[p] = found[:3]
        if d is not None:
            d[p] = found[3]
        if f is not None:
            g[p] = found[4]

    planes(low, high, values, store, group)


def neighbours(p, k, cy, cz, v):
    here, centre, y, z = k[p], v[p], cy[p], cz[p]
    total = (k[p - 1] + here) * v[p - 1] + (here + k[p + 1]) * v[p + 1]
    total = total + y * after(centre, 0) + before(y * centre, 0)
    total = total + z * after(centre, 1) + before(z * centre, 1)
    return total, centre


def own_neighbours(p, k, cy, cz, v):
    rows, lanes = slice(0, 32), slice(0, 128)
    here = k[p, rows, lanes]
    total = (k[p - 1, rows, lanes] + here) * v[p - 1, rows, lanes]
    total = total + (here + k[p + 1, rows, lanes]) * v[p + 1, rows, lanes]
    centre, y = v[p, :, lanes], cy[p, :, lanes]
    total = total + (y * after(centre, 0) + before(y * centre, 0))[rows]
    across, z = v[p, rows], cz[p, rows]
    total = total + (z * after(across, 1) + before(z * across, 1))[:, lanes]
    return total, centre[rows]


def sweep(low, high, group, k, w, g, cy, cz, v, out):
    def values(p):
        total, centre = neighbours(p, k, cy, cz, v)
        return KEEP * centre + g[p] + w[p] * total

    def store(p, value):
        out[p] = value

    planes(low, high, values, store, group)


def reach(p):
    away = max(0, 4 - p, p - 19)
    return max(0, 3 - away), 4 - away


def row_table():
    table, base = [], 0
    for p in range(24):
        three, four = reach(p)
        table.append((base, base + three, base + 2 * three))
        base += 2 * three + four
    return table, base


ROWS, ROW_COUNT = row_table()


def pack_y_kernel(f, k, m, xl, xr, up, down):
    for p in range(24):
        if p < 4:
            refs = ((xl, p - 1), (xl, 2 + p), (xl, 6 + p))
        elif p < 20:
            refs = ((f, p - 4), (m, p - 4), (k, p - 4))
        else:
            refs = ((xr, p - 20), (xr, p - 17), (xr, p - 14))
        for a, (ref, plane) in enumerate(refs):
            count, base = reach(p)[a // 2], ROWS[p][a]
            if count:
                up[base : base + count] = ref[plane, 32 - count : 32]
                down[base : base + count] = ref[plane, 0:count]


def pack_z_kernel(f, k, m, xl, xr, yl, yr, fa, ka, ma, up, down):
    lane = iota((40, 128), 1)
    zero = jnp.zeros((32, 128), F32)
    faces = [[None, None] for _ in range(3)]
    for p in range(24):
        g, i = p // 16, p % 16
        if p < 4:
            own = (xl[p - 1] if p else zero, xl[2 + p] if p else zero, xl[6 + p])
        elif p < 20:
            own = (f[p - 4], m[p - 4], k[p - 4])
        else:
            own = (xr[p - 20] if p < 23 else zero, xr[p - 17] if p < 23 else zero, xr[p - 14])
        for a, out in enumerate((fa, ma, ka)):
            count, base = reach(p)[a // 2], ROWS[p][a]
            out[p, 0:32] = own[a]
            out[p, 32:40] = jnp.zeros((8, 128), F32)
            if count:
                out[p, 32 : 32 + count] = yr[base : base + count]
                out[p, 40 - count : 40] = yl[base : base + count]
            moved = roll(out[p], 8 * i + 4, 1)
            faces[a][g] = moved if i == 0 else jnp.where(lane // 8 == i, moved, faces[a][g])
    front = lane % 8 < 4
    source, screening, conductivity = faces
    pairs = ((source[0], screening[0]), (source[1], screening[1]), conductivity)
    for g, (one, two) in enumerate(pairs):
        up[g] = jnp.where(front, one, roll(two, 4, 1))
        down[g] = jnp.where(front, roll(one, -4, 1), two)


def pair_matrix(columns):
    return jnp.where(iota((128, columns), 0) // 2 == iota((128, columns), 1) % 64, 0.125, 0.0)


def coarse_kernel(k, m, message, tall):
    pairs = pair_matrix(128)
    for slot, ref in enumerate((m, k)):
        for i in range(8):
            tall[32 * i : 32 * i + 32] = ref[2 * i] + ref[2 * i + 1]
        halve_and_pack(tall, pairs, message, 4 * slot)


def halve_and_pack(tall, pairs, message, first):
    lane16 = iota((16, 128), 1)
    halves = tall[pl.ds(0, 128, stride=2), :] + tall[pl.ds(1, 128, stride=2), :]
    coarse = dot(halves, pairs)
    for i in range(4):
        message[first + i] = jnp.where(
            lane16 < 64, coarse[16 * i : 16 * i + 16], coarse[16 * i + 64 : 16 * i + 80]
        )


def fine_kernel(pos, fa, ka, ma, zl, zr, message, v_out, w, g, k, cy, cz, f, m, d, tall):
    ix, iy, iz = pos[0], pos[1], pos[2]
    row = iota((40, 128), 0)
    lane = iota((40, 128), 1)
    far = ((row >= 32) & (row < 36) & (iy == 7)) | ((row >= 36) & (iy == 0))
    beside = ((lane < 4) & (iz < 7)) | ((lane >= 124) & (iz > 0))
    inner = (lane < 3) | (lane > 124)
    front = lane % 8 < 4
    ones = [jnp.where(front, zl[g], roll(zr[g], 4, 1)) for g in range(3)]
    twos = [jnp.where(front, roll(zl[g], -4, 1), zr[g]) for g in range(3)]
    faces = (ones[:2], twos[:2], (ones[2], twos[2]))
    for p in range(24):
        group, i = p // 16, p % 16
        absent = False
        if p < 4:
            absent = ix == 0
        elif p >= 20:
            absent = ix == 3
        gone = far | absent
        three = reach(p)[0]
        unknown = (row >= 32 + three) & (row < 40 - three)
        for a, (src, out) in enumerate(((fa, f), (ma, m), (ka, k))):
            if a == 1 and p in (0, 23):
                out[p] = jnp.full((40, 256), OUTSIDE, F32)
                continue
            side = roll(faces[a][group], -8 * i - 4, 1)
            own = src[p]
            fill = OUTSIDE if a == 1 else 0.0
            if a == 2:
                here, there = gone, gone | ~beside
                own, side = 0.5 * own, 0.5 * side
            else:
                here = gone | unknown
                there = here | ~(beside & inner)
            out[p, :, 0:128] = jnp.where(here, fill, own)
            out[p, :, 128:256] = jnp.where(there, fill, side)
    coefficients(1, 23, 11, k, f, m, d, w, g, cy, cz)
    sweep(2, 22, 10, k, w, g, cy, cz, g, v_out)

    def residual(p):
        total, centre = own_neighbours(p, k, cy, cz, v_out)
        return f[p, 0:32, 0:128] + total - d[p, 0:32, 0:128] * centre

    def values(i):
        return residual(2 * i + 4) + residual(2 * i + 5)

    def store(i, value):
        tall[pl.ds(pl.multiple_of(32 * i, 32), 32), :] = value

    planes(0, 8, values, store, 8)
    halve_and_pack(tall, pair_matrix(128), message, 0)


def pack_z1_kernel(count, own, yl, yr, up, down):
    lane = iota((16, 128), 1) % 64
    for b in range(4 * count):
        for part, src in enumerate((own, yr, yl)):
            acc_up = jnp.zeros((16, 128), F32)
            acc_down = jnp.zeros((16, 128), F32)
            for q in range(4):
                pair = src[4 * b + q]
                mask = (lane >= 16 * q) & (lane < 16 * q + 16)
                acc_up = jnp.where(mask, roll(pair, 16 * q - 48, 1), acc_up)
                acc_down = jnp.where(mask, roll(pair, 16 * q, 1), acc_down)
            up[b, 16 * part : 16 * part + 16] = acc_up
            down[b, 16 * part : 16 * part + 16] = acc_down


def clear(refs, low, high):
    for ref in refs:
        for p in (*range(low), *range(high, ref.shape[0])):
            ref[p] = jnp.zeros(ref.shape[1:], F32)


def outside1(iy, iz):
    row, lane = iota((48, 128), 0), iota((48, 128), 1)
    gone = ((row >= 16) & (row < 32) & (iy == 7)) | ((row >= 32) & (iy == 0))
    gone = gone | ((lane >= 64) & (lane < 80) & (iz == 7)) | ((lane >= 112) & (iz == 0))
    return gone | ((lane >= 80) & (lane < 112))


def spread1(ix, own, yl, yr, zl, zr, count, a, write):
    lane = iota((48, 128), 1)
    even = lane // 16 % 2 == 0
    for b in range(4):
        block = 8 * jnp.bitwise_xor(ix, b) + 4
        left, right = roll(zl[count * b + a], 48, 1), zr[count * b + a]
        sides = (jnp.where(even, right, left), jnp.where(even, left, right))
        for q in range(4):
            s = 4 * (count * b + a) + q
            pair = jnp.concatenate([own[s], yr[s], yl[s]], axis=0)
            for h in range(2):
                at = 16 * (q + 4 * h)
                side = roll(sides[q % 2], 64 - at, 1)
                value = jnp.where(lane < 64, roll(pair, 64 * h, 1), side)
                write(block + q + 4 * h, value)


def known2(shape):
    lane = iota(shape, 1)
    return (lane < 40) | (lane >= 120)


def to_second(tall, out, values, fill):
    def store(i, value):
        tall[pl.ds(pl.multiple_of(48 * i, 48), 48), :] = value

    planes(0, 16, lambda i: values(2 * i + 4) + values(2 * i + 5), store, 4)
    halves = tall[pl.ds(0, 384, stride=2), :] + tall[pl.ds(1, 384, stride=2), :]
    coarse = dot(halves, jnp.where(known2((128, 128)), pair_matrix(128), 0.0))
    for i in range(16):
        out[i + 4] = jnp.where(known2((24, 128)), coarse[24 * i : 24 * i + 24], fill)


def to_third(tall, small, write, values):
    for i in range(8):
        tall[24 * i : 24 * i + 24] = values(2 * i + 4) + values(2 * i + 5)
    halves = tall[pl.ds(0, 96, stride=2), :] + tall[pl.ds(1, 96, stride=2), :]
    spread = jnp.where(iota((128, 128), 0) // 2 == iota((128, 128), 1) % 16, 0.125, 0.0)
    small[0:96] = dot(halves, spread)
    group = iota((12, 128), 1) // 16
    packed = jnp.zeros((12, 128), F32)
    for i in range(8):
        packed = jnp.where(group == i, small[12 * i : 12 * i + 12], packed)
    small[0:12] = packed
    write(slice(0, 2), small[10:12])
    write(slice(2, 8), small[0:6])


def cut1(ix, src, out):
    for p in range(16):
        out[p, 0:20] = src[8 * ix + p, 0:20]
        out[p, 20:24] = src[8 * ix + p, 44:48]


def cut2(ix, src, out):
    for p in range(12):
        out[p, 0:12] = src[4 * ix + p, 0:12]
        out[p, 12:16] = src[4 * ix + p, 20:24]


def static_kernel(
    pos, own, yl, yr, zl, zr,
    coarsest, k1, w1, cy1, cz1, d1, k2, w2, cy2, cz2, d2,
    k1n, w1n, cy1n, cz1n, k2n, w2n, cy2n, cz2n,
    m1, m2, tall, small,
):
    ix, iy, iz = pos[0], pos[1], pos[2]
    gone = outside1(iy, iz)
    clear((k1, w1, cy1, cz1), 4, 36)
    clear((k2, w2, cy2, cz2), 4, 20)

    def write_m(p, value):
        m1[p] = jnp.where(gone, OUTSIDE, value)

    def write_k(p, value):
        k1[p] = jnp.where(gone, 0.0, 0.125 * value)

    spread1(ix, own, yl, yr, zl, zr, 2, 0, write_m)
    spread1(ix, own, yl, yr, zl, zr, 2, 1, write_k)
    coefficients(4, 36, 8, k1, None, m1, d1, w1, None, cy1, cz1)
    to_second(tall, m2, lambda p: m1[p], OUTSIDE)
    to_second(tall, k2, lambda p: 0.25 * k1[p], 0.0)
    coefficients(4, 20, 16, k2, None, m2, d2, w2, None, cy2, cz2)

    def write(slot):
        def put(where, value):
            coarsest[slot, where] = value

        return put

    to_third(tall, small, write(0), lambda p: m2[p])
    to_third(tall, small, write(1), lambda p: 0.25 * k2[p])
    for src, out in ((k1, k1n), (w1, w1n), (cy1, cy1n), (cz1, cz1n)):
        cut1(ix, src, out)
    for src, out in ((k2, k2n), (w2, w2n), (cy2, cy2n), (cz2, cz2n)):
        cut2(ix, src, out)


def middle_kernel(
    pos, own, yl, yr, zl, zr, coarsest, k1, w1, cy1, cz1, d1, k2, w2, cy2, cz2, d2,
    message, v1n, g1n, v2n, g2n,
    f1, g1, v1, f2, g2, v2, tall, small,
):
    ix, iy, iz = pos[0], pos[1], pos[2]
    gone = outside1(iy, iz)
    clear((g1, v1), 4, 36)
    clear((g2, v2), 4, 20)

    def write(p, value):
        value = jnp.where(gone, 0.0, value)
        f1[p] = value
        g1[p] = w1[p] * value

    spread1(ix, own, yl, yr, zl, zr, 1, 0, write)
    sweep(4, 36, 16, k1, w1, g1, cy1, cz1, g1, v1)

    def residual1(p):
        total, centre = neighbours(p, k1, cy1, cz1, v1)
        return jnp.where(gone, 0.0, f1[p] + total - d1[p] * centre)

    to_second(tall, f2, residual1, 0.0)
    for p in range(4, 20):
        g2[p] = w2[p] * f2[p]
    sweep(4, 20, 16, k2, w2, g2, cy2, cz2, g2, v2)
    row24 = iota((24, 128), 0)
    gone2 = ((row24 >= 8) & (row24 < 16) & (iy == 7)) | ((row24 >= 16) & (iy == 0))

    def residual2(p):
        total, centre = neighbours(p, k2, cy2, cz2, v2)
        return jnp.where(gone2, 0.0, f2[p] + total - d2[p] * centre)

    def put(where, value):
        message[0, where] = value

    to_third(tall, small, put, residual2)
    message[1] = coarsest[0]
    message[2] = coarsest[1]
    cut1(ix, v1, v1n)
    cut1(ix, g1, g1n)
    cut2(ix, v2, v2n)
    cut2(ix, g2, g2n)


def duplicate(out, base, rows, first, count):
    value = rows[first : first + count]
    out[pl.ds(base, count, stride=2), :] = value
    out[pl.ds(base + 1, count, stride=2), :] = value


def last_kernel(
    pos, own, first, second, v0, w0, g0, k0, cy0, cz0, v1, g1, v2, g2, k1, w1, cy1, cz1, k2, w2, cy2, cz2,
    out,
    k3, f3, m3, w3, g3, cy3, cz3, a3, rows, dup, a2, b2, a1, b1, wide, low, high, a0, b0,
):
    ix, iy, iz = pos[0], pos[1], pos[2]
    row = iota((24, 128), 0) + 4 * iy - 10
    lane = iota((24, 128), 1)
    gone = (row < 0) | (row >= 32) | ((lane >= 32) & (lane < 112))
    gone = gone | ((lane >= 16) & (lane < 32) & (iz == 7)) | ((lane >= 112) & (iz == 0))
    clear((k3, g3, a3), 2, 10)
    crossed = (iy // 2) % 2 == 0

    def stack(index):
        one, two = first[index], second[index]
        ahead, behind = jnp.where(crossed, two, one), jnp.where(crossed, one, two)
        ahead = jnp.where(iy == 1, roll(ahead, 4, 0), ahead)
        behind = jnp.where(iy == 6, roll(behind, 4, 0), behind)
        return jnp.concatenate([ahead, own[index], behind], axis=0)

    for a, (ref, fill) in enumerate(((f3, 0.0), (m3, OUTSIDE), (k3, 0.0))):
        here, left, right = (stack(3 * z + a) for z in range(3))
        for x in range(8):
            value = jnp.where(
                lane < 16,
                roll(here, -16 * x, 1),
                jnp.where(lane < 64, roll(right, 16 - 16 * x, 1), roll(left, 112 - 16 * x, 1)),
            )
            ref[x + 2] = jnp.where(gone, fill, value)
    coefficients(2, 10, 8, k3, f3, m3, None, w3, g3, cy3, cz3)
    field = [g3[p] for p in range(1, 11)]
    for _ in range(COARSE_SWEEPS - 1):
        inner = []
        for p in range(2, 10):
            behind, here, ahead = field[p - 2 : p + 1]
            total, _ = neighbours(p, k3, cy3, cz3, {p: here, p - 1: behind, p + 1: ahead})
            inner.append(KEEP * here + g3[p] + w3[p] * total)
        field = [field[0], *inner, field[9]]
    for p in range(8):
        a3[p + 2] = field[p + 1]

    src, column = iota((128, 128), 0), iota((128, 128), 1)
    to2 = jnp.where(
        ((column < 40) & (src == column // 2)) | ((column >= 120) & (src == 64 + column // 2)), 1.0, 0.0
    )
    for x in range(6):
        rows[24 * x : 24 * x + 24] = a3[2 * ix + x]
    rows[0:144] = dot(rows[0:144], to2)
    for x in range(6):
        duplicate(dup, 16 * x, rows, 24 * x + 10, 6)
        duplicate(dup, 16 * x + 12, rows, 24 * x + 8, 2)
        both = dup[16 * x : 16 * x + 16]
        a2[2 * x] = v2[2 * x] + both
        a2[2 * x + 1] = v2[2 * x + 1] + both
    sweep(1, 11, 10, k2, w2, g2, cy2, cz2, a2, b2)
    sweep(2, 10, 8, k2, w2, g2, cy2, cz2, b2, a2)

    to1 = jnp.where(
        ((column < 80) & (src == column // 2)) | ((column >= 112) & (src == 64 + column // 2)), 1.0, 0.0
    )
    for x in range(8):
        rows[16 * x : 16 * x + 16] = a2[x + 2]
    rows[0:128] = dot(rows[0:128], to1)
    for x in range(8):
        duplicate(dup, 24 * x, rows, 16 * x, 10)
        duplicate(dup, 24 * x + 20, rows, 16 * x + 14, 2)
        both = dup[24 * x : 24 * x + 24]
        a1[2 * x] = v1[2 * x] + both
        a1[2 * x + 1] = v1[2 * x + 1] + both
    sweep(2, 14, 12, k1, w1, g1, cy1, cz1, a1, b1)
    sweep(3, 13, 10, k1, w1, g1, cy1, cz1, b1, a1)

    to0 = jnp.where(iota((128, 256), 0) == iota((128, 256), 1) // 2, 1.0, 0.0)
    for x in range(10):
        rows[24 * x : 24 * x + 24] = a1[x + 3]
    wide[...] = dot(rows[0:240], to0)
    for x in range(10):
        for half, lanes in ((low, slice(0, 128)), (high, slice(128, 256))):
            mid = wide[24 * x : 24 * x + 18, lanes]
            half[pl.ds(0, 18, stride=2), :] = mid
            half[pl.ds(1, 18, stride=2), :] = mid
            ahead = wide[24 * x + 22 : 24 * x + 24, lanes]
            half[pl.ds(36, 2, stride=2), :] = ahead
            half[pl.ds(37, 2, stride=2), :] = ahead
            for p in (2 * x + 2, 2 * x + 3):
                a0[p, :, lanes] = v0[p, :, lanes] + half[0:40]
    sweep(3, 21, 9, k0, w0, g0, cy0, cz0, a0, b0)

    def values(p):
        total, centre = own_neighbours(p, k0, cy0, cz0, b0)
        return KEEP * centre + g0[p, 0:32, 0:128] + w0[p, 0:32, 0:128] * total

    def store(p, value):
        out[p - 4] = value

    planes(4, 20, values, store, 16)


VMEM = pl.BlockSpec(memory_space=pltpu.VMEM)
SMEM = pl.BlockSpec(memory_space=pltpu.SMEM)


COARSE_TARGETS = ((2, 3, 0, 1, 6, 7, 4, 5), (1, 0, 4, 5, 2, 3, 7, 6))


def call(kernel, outs, scratch, *args, pos=None):
    specs = [VMEM] * len(args)
    if pos is not None:
        args = (pos,) + args
        specs = [SMEM] + specs
    return pl.pallas_call(
        kernel,
        out_shape=[jax.ShapeDtypeStruct(s, F32) for s in outs],
        in_specs=specs,
        out_specs=[VMEM] * len(outs),
        scratch_shapes=[pltpu.VMEM(s, F32) for s in scratch],
        compiler_params=pltpu.CompilerParams(vmem_limit_bytes=16 * 1024 * 1024),
        name=getattr(kernel, "__name__", "pack_z1_kernel"),
    )(*args)


def swap(x, axis, bits):
    size = lax.axis_size(axis)
    return lax.ppermute(x, axis, [(i, i ^ bits) for i in range(size)])


FULL, SIDES = (24, 40, 256), (3, 40, 128)
ONE, TWO, THREE = (40, 48, 128), (24, 24, 128), (12, 24, 128)
NEAR1, NEAR2 = (16, 24, 128), (12, 16, 128)
TALL = (768, 128)


def gather_x(x):
    return jnp.concatenate([x] + [swap(x, "gx", bits) for bits in (1, 2, 3)])


def both_sides(up, down, axis):
    size = lax.axis_size(axis)
    even = lax.axis_index(axis) % 2 == 0
    far = [(i, (i + 1) % size if i % 2 else (i - 1) % size) for i in range(size)]
    there = lax.ppermute(jnp.where(even, down, up), axis, far)
    here = swap(jnp.where(even, up, down), axis, 1)
    return jnp.where(even, there, here), jnp.where(even, here, there)


def pack_z1(count, own, yl, yr):
    kernel = functools.partial(pack_z1_kernel, count)
    return call(kernel, [(4 * count, 48, 128)] * 2, [], own, yl, yr)


def ordered(x, *others):
    return lax.optimization_barrier((x, *others))[0]


def per_device(f, k, m):
    pos = jnp.stack([lax.axis_index("gx"), lax.axis_index("gy"), lax.axis_index("gz")])
    pos = pos.astype(jnp.int32)

    up = jnp.concatenate([f[13:], m[13:], k[12:]])
    down = jnp.concatenate([f[:3], m[:3], k[:4]])
    xl, xr = both_sides(up, down, "gx")
    (brick,) = call(
        coarse_kernel, [(8, 16, 128)], [(256, 128)], k, m
    )
    static = gather_x(brick)

    yl, yr = both_sides(*call(pack_y_kernel, [(ROW_COUNT, 128)] * 2, [], f, k, m, xl, xr), "gy")
    fa, ka, ma, up, down = call(
        pack_z_kernel, [(24, 40, 128)] * 3 + [SIDES] * 2, [], f, k, m, xl, xr, yl, yr
    )
    zl, zr = both_sides(up, down, "gz")
    static_yl, static_yr = both_sides(static, static, "gy")
    brick, *level0 = call(
        fine_kernel,
        [(4, 16, 128)] + [FULL] * 6,
        [FULL] * 3 + [(256, 128)],
        fa, ka, ma, zl, zr,
        pos=pos,
    )
    static_up, static_down = pack_z1(2, static, static_yl, static_yr)

    own = gather_x(brick)
    static_zl, static_zr = both_sides(static_up, static_down, "gz")
    coarsest, *static = call(
        static_kernel,
        [(2, 8, 128)] + [ONE] * 5 + [TWO] * 5 + [NEAR1] * 4 + [NEAR2] * 4,
        [ONE, TWO, TALL, (96, 128)],
        static, static_yl, static_yr, static_zl, static_zr,
        pos=pos,
    )
    whole, near = static[:10], static[10:]
    yl, yr = both_sides(own, own, "gy")
    up, down = pack_z1(1, own, yl, yr)
    zl, zr = both_sides(up, down, "gz")
    message, *vary = call(
        middle_kernel,
        [(3, 8, 128)] + [NEAR1] * 2 + [NEAR2] * 2,
        [ONE] * 3 + [TWO] * 3 + [TALL, (96, 128)],
        own, yl, yr, zl, zr, coarsest, *whole,
        pos=pos,
    )

    own = jnp.concatenate([message, *both_sides(message, message, "gz")])
    first, second = (lax.ppermute(own, "gy", list(enumerate(t))) for t in COARSE_TARGETS)
    return call(
        last_kernel,
        [(16, 32, 128)],
        [THREE] * 8 + [(240, 128), (224, 128)] + [NEAR2] * 2 + [NEAR1] * 2
        + [(240, 256), (64, 128), (64, 128)] + [FULL] * 2,
        own, first, second, *level0, *vary, *near,
        pos=pos,
    )[0]


def solution(mesh):
    placed = (P("gx", "gy", "gz"), P("gx", "gy", "gz"), P("gx", "gy", "gz"))
    return jax.shard_map(
        per_device, mesh=mesh, in_specs=placed, out_specs=P("gx", "gy", "gz"), check_vma=False
    )
```
